32 devices in a mesh: section: 2 (over x), dp: 4 (over y, core), mp: 4 (over z).
Axes of the slice: x: 2, y: 2, z: 4, core: 2. Of those that a mesh axis runs over, the one named last changes fastest.
Arguments:
- layer_in: bfloat16 [2, 8, 1024, 512], P('section', 'dp', 'mp'), may hold values from -6 to 6
- segment_ids: int32 [2, 8, 1024], P(None, 'dp'), may hold values from 0 to 3, never falling along the last dimension, each value on 1 to 769 neighbouring positions
- out_grads: bfloat16 [2, 8, 1024, 512], P('section', 'dp', 'mp'), may hold values from -6 to 6
- w_qkv: bfloat16 [2, 512, 3, 512], P('section', 'dp', None, 'mp'), may hold values from -0.25 to 0.25
- w_out: bfloat16 [2, 512, 512], P('section', 'mp', 'dp'), may hold values from -2 to 2
- w_up: bfloat16 [2, 512, 2048], P('section', 'dp', 'mp'), may hold values from -0.25 to 0.25
- w_down: bfloat16 [2, 2048, 512], P('section', 'mp', 'dp'), may hold values from -0.125 to 0.125
- norm_gain: float32 [2, 3, 512], P('section', None, ('dp', 'mp')), may hold values from 0.5 to 1.5
- norm_bias: float32 [2, 3, 512], P('section', None, ('dp', 'mp')), may hold values from -1.2 to 1.2
- w_qc: bfloat16 [512, 512], P('dp', ('section', 'mp')), may hold values from -0.25 to 0.25
- w_kvc: bfloat16 [512, 2, 512], P('dp', None, ('section', 'mp')), may hold values from -0.25 to 0.25
- w_oc: bfloat16 [512, 512], P(('section', 'mp'), 'dp'), may hold values from -2 to 2
Outputs:
- section_out: bfloat16 [2, 8, 1024, 512], P('section', 'dp', 'mp')
- in_grads: bfloat16 [2, 8, 1024, 512], P('section', 'dp', 'mp')
- grad_qkv: float32 [2, 512, 3, 512], P('section', 'dp', None, 'mp')
- grad_out: float32 [2, 512, 512], P('section', 'mp', 'dp')
- grad_up: float32 [2, 512, 2048], P('section', 'dp', 'mp')
- grad_down: float32 [2, 2048, 512], P('section', 'mp', 'dp')
- grad_gain: float32 [2, 3, 512], P('section', None, ('dp', 'mp'))
- grad_bias: float32 [2, 2, 512], P('section', None, ('dp', 'mp'))
- grad_ffn_bias: float32 [2, 512], P('section', ('dp', 'mp'))
- grad_qc: float32 [512, 512], P('dp', ('section', 'mp'))
- grad_kvc: float32 [512, 2, 512], P('dp', None, ('section', 'mp'))
- grad_oc: float32 [512, 512], P(('section', 'mp'), 'dp')
The draws below stay inside these ranges and needn't reach their ends.
Inputs may be any that keep to these rules, and one draw needn't show every extreme that they name: `segment_ids`: in every row of both layers the segment numbers start at 0 and never fall, all 4 occur, and one segment has 769 positions.
All inputs are finite; a program needn't handle non-finite values.
Results may differ from the reference program's by a relative error of at most 0.035.
Values may be sent and summed in bfloat16 or wider, within the bound.
No kernel may reach another device: no remote copies, remote signals or barrier semaphores. Data moves between devices by JAX's collectives and lax.ppermute only.
A program may use at most 192 MiB of HBM per device.

```python
import math
import jax
import jax.numpy as jnp
import numpy as np
from jax import lax

D = 512
FF = 2048
HEADS = 8
HD = 64
LEN = 1024
SEGS = 4
ROWS_ALL = 8


def level_of(rng, extent, split, least, high):
    level, own = 1.0, jax.random.fold_in(rng, 6)
    for position, shards_of in split:
        draws = jnp.exp(jax.random.uniform(jax.random.fold_in(own, position), (shards_of,), jnp.float32, least / len(split), high / len(split)))
        level = level * jnp.repeat(draws, extent[position] // shards_of).reshape([-1 if axis == position else 1 for axis in range(len(extent))])
    return level


def split_up(number_of, total, reach, skew):
    loads = [(1 << 20) // math.isqrt(grade ** skew) + 1 for grade in range(2, number_of + 1)]
    surplus, given = total - reach - (number_of - 1), [1] * (number_of - 1)
    while surplus > 0:
        movable = [i for i in range(number_of - 1) if given[i] < reach]
        mass, left = sum([loads[i] for i in movable]), surplus
        for i in movable:
            more = min(reach - given[i], max(1, left * loads[i] // mass), surplus)
            given[i] = given[i] + more
            surplus = surplus - more
    return np.array([reach] + given)


def uneven(key, count, total, limit, skew):
    if count == 2:
        one = jax.random.randint(key, (), max(1, total - limit), min(limit, total - 1) + 1)
        return jnp.stack([one, total - one])
    lengths = jnp.asarray(split_up(count, total, limit, skew), jnp.int32)
    pairs = (count - 1) // 2
    donor, taker = lengths[1:1 + 2 * pairs:2], lengths[2:2 + 2 * pairs:2]
    room = jnp.minimum(donor - 1, limit - taker)
    passed = jax.random.randint(jax.random.fold_in(key, 1), (pairs,), 0, 1 << 20) % (room + 1)
    lengths = lengths.at[1:1 + 2 * pairs:2].set(donor - passed).at[2:2 + 2 * pairs:2].set(taker + passed)
    return lengths[jax.random.permutation(jax.random.fold_in(key, 2), count)]


def gaussian(own_key, extent, width, reach, split=(), dtype=jnp.bfloat16):
    entries = jax.random.normal(own_key, extent, jnp.float32) * width
    if len(split) > 0:
        entries = level_of(own_key, extent, split, -0.22, 0.18) * entries
    return jnp.clip(entries, min=-reach, max=reach).astype(dtype)


def setup_inputs(seed: int = 0) -> dict:
    arg_keys = jax.random.split(jax.random.key(seed), 13)
    return {
        "layer_in": gaussian(arg_keys[0], (2, ROWS_ALL, LEN, D), 1.0, 6.0, ((0, 2), (1, 4), (2, 4))),
        "segment_ids": jax.vmap(lambda own: jnp.searchsorted(jnp.cumsum(uneven(own, SEGS, LEN, 3 * LEN // 4 + 1, 0)), jnp.arange(LEN), side="right"))(jax.random.split(arg_keys[1], 2 * ROWS_ALL)).reshape((2, ROWS_ALL, LEN)).astype(jnp.int32),
        "out_grads": gaussian(arg_keys[2], (2, ROWS_ALL, LEN, D), 1.0, 6.0, ((0, 2), (1, 4), (2, 4))),
        "w_qkv": gaussian(arg_keys[3], (2, D, 3, D), D ** -0.5, 0.25, ((0, 2), (1, 4), (3, 4))),
        "w_out": gaussian(arg_keys[4], (2, D, D), (D // 64) ** -0.5, 2.0, ((0, 2), (1, 4), (2, 4))),
        "w_up": gaussian(arg_keys[5], (2, D, FF), D ** -0.5, 0.25, ((0, 2), (1, 4), (2, 4))),
        "w_down": gaussian(arg_keys[6], (2, FF, D), FF ** -0.5, 0.125, ((0, 2), (1, 4), (2, 4))),
        "norm_gain": jnp.clip(1.0 + 0.1 * jax.random.normal(arg_keys[7], (2, 3, D), jnp.float32), 0.5, 1.5),
        "norm_bias": gaussian(arg_keys[8], (2, 3, D), 0.2, 1.2, ((0, 2), (2, 16)), jnp.float32),
        "w_qc": gaussian(arg_keys[9], (D, D), D ** -0.5, 0.25, ((0, 4), (1, 8))),
        "w_kvc": gaussian(arg_keys[10], (D, 2, D), D ** -0.5, 0.25, ((0, 4), (2, 8))),
        "w_oc": gaussian(arg_keys[11], (D, D), (D // 64) ** -0.5, 2.0, ((0, 8), (1, 4))),
    }


@jax.custom_vjp
def low(v):
    return lax.optimization_barrier(v.astype(jnp.bfloat16)).astype(jnp.float32)

@jax.custom_vjp
def low_back(v):
    return v

def low_keep(v):
    return (low(v), None)

def low_pass(kept, grad):
    return (grad,)

def back_keep(v):
    return (v, None)

def back_low(kept, grad):
    return (low(grad),)
low.defvjp(low_keep, low_pass)
low_back.defvjp(back_keep, back_low)
EPS = 1e-05
NEG = -1e+30

def round_both(inputs):
    return low(low_back(inputs))

def precise(left_side, right_side):
    return jnp.dot(left_side, right_side, precision=lax.Precision.HIGHEST)

def normalize(states, gain_vec, bias_vec):
    average = lax.optimization_barrier(jnp.mean(states, axis=-1, keepdims=True))
    centred = states - average
    spread = lax.optimization_barrier(jnp.mean(centred * centred, axis=-1, keepdims=True))
    return centred * lax.rsqrt(spread + EPS) * gain_vec + bias_vec

def attend(queries, key_rows, value_rows, matches):
    factor = HD ** (-0.5)
    scores = low_back(jnp.einsum('qhe,khe->hqk', queries, key_rows, precision=lax.Precision.HIGHEST) * factor)
    scores = jnp.where(matches[None], scores, NEG)
    highest = lax.optimization_barrier(jnp.max(scores, axis=-1, keepdims=True))
    weights = jnp.exp(scores - highest)
    chances = weights / lax.optimization_barrier(jnp.sum(weights, axis=-1, keepdims=True))
    attended = jnp.einsum('hqk,khe->qhe', low(chances), value_rows, precision=lax.Precision.HIGHEST)
    return round_both(attended.reshape(attended.shape[0], -1))

def self_attention(states, gain_vec, bias_vec, qkv_weight, out_weight, matches):
    normed = low(normalize(states, gain_vec, bias_vec))
    qkv = round_both(precise(normed, qkv_weight.reshape(D, 3 * D))).reshape(-1, 3, HEADS, HD)
    attended = attend(qkv[:, 0], qkv[:, 1], qkv[:, 2], matches)
    return states + low_back(precise(attended, out_weight))

def feed_forward(states, gain_vec, bias_vec, up_weight, down_weight):
    normed = low(normalize(states, gain_vec, bias_vec))
    hidden = low(jax.nn.gelu(low_back(precise(normed, up_weight)), approximate=False))
    return states + low_back(precise(hidden, down_weight))

def cross_attention(states, gain_vec, bias_vec, memory, query_weight, pair_weight, cross_weight, matches):
    normed = low(normalize(states, gain_vec, bias_vec))
    queries = round_both(precise(normed, query_weight)).reshape(-1, HEADS, HD)
    pairs = round_both(precise(memory, pair_weight.reshape(D, 2 * D))).reshape(-1, 2, HEADS, HD)
    attended = attend(queries, pairs[:, 0], pairs[:, 1], matches)
    return states + low_back(precise(attended, cross_weight))

def layer_pair(source, target, source_segs, target_segs, params):
    qkv_w, out_w, up_w, down_w, gains, biases, query_w, pair_w, cross_w = params
    source_match = source_segs[:, None] == source_segs[None, :]
    target_match = target_segs[:, None] == target_segs[None, :]
    cross_match = target_segs[:, None] == source_segs[None, :]
    encoded = self_attention(source, gains[0, 0], biases[0, 0], qkv_w[0], out_w[0], source_match)
    encoded = feed_forward(encoded, gains[0, 1], biases[0, 1], up_w[0], down_w[0])
    memory = low(normalize(encoded, gains[0, 2], biases[0, 2]))
    middle = self_attention(target, gains[1, 0], biases[1, 0], qkv_w[1], out_w[1], target_match)
    joined = cross_attention(middle, gains[1, 2], biases[1, 2], memory, query_w, pair_w, cross_w, cross_match)
    decoded = feed_forward(joined, gains[1, 1], biases[1, 1], up_w[1], down_w[1])
    return (memory, decoded)

def reference(layer_in, segment_ids, out_grads, w_qkv, w_out, w_up, w_down, norm_gain, norm_bias, w_qc, w_kvc, w_oc):
    params = tuple((argument.astype(jnp.float32) for argument in (w_qkv, w_out, w_up, w_down, norm_gain, norm_bias, w_qc, w_kvc, w_oc)))
    inputs = layer_in.astype(jnp.float32)
    cotangents = out_grads.astype(jnp.float32)
    one_step = jax.checkpoint(layer_pair)

    def whole_forward(states, weights):

        def scan_step(running, pieces):
            return (running, one_step(pieces[0], pieces[1], pieces[2], pieces[3], weights))
        _, (memory, decoded) = lax.scan(scan_step, jnp.zeros((), jnp.float32), (states[0], states[1], segment_ids[0], segment_ids[1]))
        return jnp.stack([memory, decoded])
    outputs, pullback = jax.vjp(whole_forward, inputs, params)
    grad_in, grad_params = pullback(cotangents)
    bias_all = grad_params[5]
    bias_attn = jnp.stack([bias_all[:, 0], bias_all[:, 2]], axis=1)
    bias_ffn = bias_all[:, 1]
    return (outputs.astype(jnp.bfloat16), grad_in.astype(jnp.bfloat16), grad_params[0], grad_params[1], grad_params[2], grad_params[3], grad_params[4], bias_attn, bias_ffn, grad_params[6], grad_params[7], grad_params[8])
```

```python
import jax
import jax.numpy as jnp
from jax import lax
from jax.sharding import PartitionSpec as P

HD = 64
EPS = 1e-05
NEG = -1e30
BF = jnp.bfloat16
F32 = jnp.float32


def swap(block, axis, bit):
    count = lax.axis_size(axis)
    return lax.ppermute(block, axis, [(i, i ^ bit) for i in range(count)])


def oneway(block, axis, source, target):
    return lax.ppermute(block, axis, [(source, target)])


def dp_bits():
    count = lax.axis_size("dp")
    return [1 << b for b in range(1, count.bit_length() - 1)]


def gather_blocks(shard):
    ways = lax.axis_size("mp")
    tiled = jnp.broadcast_to(shard[None], (ways,) + shard.shape)
    blocks = [(0, lax.all_to_all(tiled, "mp", 0, 0, tiled=True))]
    for bit in dp_bits():
        blocks = blocks + [(a ^ bit, swap(b, "dp", bit)) for a, b in blocks]
    return blocks + [(a ^ 1, swap(b, "dp", 1)) for a, b in blocks]


def relative_order():
    order = [0]
    for bit in dp_bits():
        order = order + [a ^ bit for a in order]
    return order + [a ^ 1 for a in order]


def assemble(blocks):
    order = {a: b for a, b in blocks}
    stacked = jnp.stack([order[a] for a in range(len(blocks))])
    me = lax.axis_index("dp")
    stacked = jnp.take(stacked, jnp.arange(len(blocks)) ^ me, axis=0)
    count, ways, blk, cols = stacked.shape
    return stacked.transpose(1, 0, 2, 3).reshape(ways, count * blk, cols)


def to_relative(grad):
    count = lax.axis_size("dp")
    ways, depth, cols = grad.shape
    me = lax.axis_index("dp")
    tiles = grad.astype(BF).reshape(ways, count, depth // count, cols).transpose(1, 0, 2, 3)
    return jnp.take(tiles, jnp.array(relative_order()) ^ me, axis=0)


def reduce_blocks(grad):
    for bit in [1] + dp_bits()[::-1]:
        half = grad.shape[0] // 2
        other = swap(grad[half:], "dp", bit)
        grad = (grad[:half].astype(F32) + other.astype(F32)).astype(BF)
    parts = lax.all_to_all(grad[0], "mp", 0, 0, tiled=True)
    return jnp.sum(parts.astype(F32), axis=0)


def rows_in(local, core):
    rows, span, width = local.shape
    halves = local.reshape(rows, 2, span // 2, width)
    first = core == 0
    keep = jnp.where(first, halves[:, 0], halves[:, 1])
    send = jnp.where(first, halves[:, 1], halves[:, 0])
    other = swap(send, "dp", 1)
    chip = jnp.where(first, jnp.concatenate([keep, other]), jnp.concatenate([other, keep]))
    return lax.all_to_all(chip, "mp", 0, 0, tiled=True).reshape(-1, width)


def rows_out(own, core, rows):
    width = own.shape[-1]
    ways = lax.axis_size("mp")
    chip = lax.all_to_all(own.reshape(ways, -1, width), "mp", 0, 0, tiled=True)
    first = core == 0
    keep = jnp.where(first, chip[:rows], chip[rows:])
    send = jnp.where(first, chip[rows:], chip[:rows])
    other = swap(send, "dp", 1)
    low = jnp.where(first, keep, other)
    high = jnp.where(first, other, keep)
    return jnp.concatenate([low, high], axis=1)


def stats(states):
    average = jnp.mean(states, axis=-1, keepdims=True)
    centred = states - average
    inv = lax.rsqrt(jnp.mean(centred * centred, axis=-1, keepdims=True) + EPS)
    return centred * inv, inv


def norm_fwd(states, gain, bias):
    hat, _ = stats(states)
    return (hat * gain + bias).astype(BF)


def norm_bwd(states, gain, grad):
    hat, inv = stats(states)
    e = grad * gain
    dx = inv * (
        e - jnp.mean(e, axis=-1, keepdims=True) - hat * jnp.mean(e * hat, axis=-1, keepdims=True)
    )
    return dx, jnp.sum(grad * hat, axis=0), jnp.sum(grad, axis=0)


def mm(a, b):
    return jnp.dot(a, b, preferred_element_type=F32)


def nt(a, b):
    return lax.dot_general(a, b, (((1,), (1,)), ((), ())), preferred_element_type=F32)


def tn(a, b):
    return lax.dot_general(a, b, (((0,), (0,)), ((), ())), preferred_element_type=F32)


def heads(x):
    return x.reshape(x.shape[0], -1, HD)


def attn_fwd(q, k, v, seg_q, seg_k):
    s = jnp.einsum("qhe,khe->hqk", heads(q), heads(k), preferred_element_type=F32) * HD**-0.5
    s = jnp.where((seg_q[:, None] == seg_k[None, :])[None], s, NEG)
    top = jnp.max(s, axis=-1, keepdims=True)
    w = jnp.exp(s - top)
    total = jnp.sum(w, axis=-1, keepdims=True)
    p = (w / total).astype(BF)
    o = jnp.einsum("hqk,khe->qhe", p, heads(v), preferred_element_type=F32)
    return o.astype(BF).reshape(q.shape), (top + jnp.log(total))[..., 0]


def attn_bwd(q, k, v, seg_q, seg_k, lse, do):
    s = jnp.einsum("qhe,khe->hqk", heads(q), heads(k), preferred_element_type=F32) * HD**-0.5
    s = jnp.where((seg_q[:, None] == seg_k[None, :])[None], s, NEG)
    p = jnp.exp(s - lse[..., None])
    dp = jnp.einsum("qhe,khe->hqk", heads(do), heads(v), preferred_element_type=F32)
    ds = (p * (dp - jnp.sum(p * dp, axis=-1, keepdims=True))).astype(BF)
    dq = jnp.einsum("hqk,khe->qhe", ds, heads(k), preferred_element_type=F32) * HD**-0.5
    dk = jnp.einsum("hqk,qhe->khe", ds, heads(q), preferred_element_type=F32) * HD**-0.5
    dv = jnp.einsum("hqk,qhe->khe", p.astype(BF), heads(do), preferred_element_type=F32)
    return (
        dq.astype(BF).reshape(q.shape),
        dk.astype(BF).reshape(k.shape),
        dv.astype(BF).reshape(k.shape),
    )


def cols(weight, at):
    ways, depth, _ = weight.shape
    return weight[:, :, at * 128 : at * 128 + 128].transpose(1, 0, 2).reshape(depth, ways * 128)


def pack(parts, ways):
    depth = parts[0].shape[0]
    return jnp.concatenate(
        [p.reshape(depth, ways, -1).transpose(1, 0, 2) for p in parts], axis=-1
    )


def self_fwd(x_full, seg, w1, gain, bias):
    own = x_full.shape[0] // 2
    normed = norm_fwd(x_full.astype(F32), gain, bias)
    q = mm(normed[:own], cols(w1, 0)).astype(BF)
    k = mm(normed, cols(w1, 1)).astype(BF)
    v = mm(normed, cols(w1, 2)).astype(BF)
    att, lse = attn_fwd(q, k, v, seg[:own], seg)
    mid = x_full[:own].astype(F32) + nt(att, cols(w1, 3))
    return normed, q, k, v, att, lse, mid


def self_bwd(d_mid, normed, q, k, v, att, lse, seg, w1):
    own = q.shape[0]
    ways = w1.shape[0]
    low = d_mid.astype(BF)
    d_out = tn(low, att)
    d_att = mm(low, cols(w1, 3)).astype(BF)
    dq, dk, dv = attn_bwd(q, k, v, seg[:own], seg, lse, d_att)
    grads = pack([tn(normed[:own], dq), tn(normed, dk), tn(normed, dv), d_out], ways)
    d_normed = nt(dk, cols(w1, 1)) + nt(dv, cols(w1, 2))
    return nt(dq, cols(w1, 0)) + d_normed[:own], d_normed[own:].astype(BF), grads


def up_down(w2):
    ways, depth, both = w2.shape
    half = both // 2
    up = w2[:, :, :half].transpose(1, 0, 2).reshape(depth, ways * half)
    down = w2[:, :, half:].transpose(1, 0, 2).reshape(depth, ways * half)
    return up, down


def feed_fwd(states, w2, gain, bias):
    up, down = up_down(w2)
    normed = norm_fwd(states, gain, bias)
    pre = mm(normed, up)
    cdf = 0.5 * (1.0 + lax.erf(pre * 0.5**0.5))
    hidden = (pre * cdf).astype(BF)
    slope = (cdf + pre * jnp.exp(-0.5 * pre * pre) * 0.3989422804014327).astype(BF)
    return states + nt(hidden, down), hidden, slope


def feed_bwd(states, cot, hidden, slope, w2, gain, bias):
    up, down = up_down(w2)
    normed = norm_fwd(states, gain, bias)
    low = cot.astype(BF)
    d_down = tn(low, hidden)
    d_pre = (mm(low, down) * slope.astype(F32)).astype(BF)
    d_up = tn(normed, d_pre)
    dx, d_gain, d_bias = norm_bwd(states, gain, nt(d_pre, up))
    return cot + dx, pack([d_up, d_down], w2.shape[0]), d_gain, d_bias


def cross_both(mid, mem, cot, seg_q, seg_k, w2, w3, gains, biases):
    ways = w3.shape[0]
    cross_in = norm_fwd(mid, gains[2], biases[2])
    q = mm(cross_in, cols(w3, 0)).astype(BF)
    k = mm(mem, cols(w3, 1)).astype(BF)
    v = mm(mem, cols(w3, 2)).astype(BF)
    att, lse = attn_fwd(q, k, v, seg_q, seg_k)
    joined = mid + nt(att, cols(w3, 3))
    decoded, hidden, slope = feed_fwd(joined, w2, gains[1], biases[1])
    d_joined, grad2, dg1, db1 = feed_bwd(joined, cot, hidden, slope, w2, gains[1], biases[1])
    low = d_joined.astype(BF)
    d_oc = tn(low, att)
    d_att = mm(low, cols(w3, 3)).astype(BF)
    dq, dk, dv = attn_bwd(q, k, v, seg_q, seg_k, lse, d_att)
    grad3 = pack([tn(cross_in, dq), tn(mem, dk), tn(mem, dv), d_oc], ways)
    d_mem = (nt(dk, cols(w3, 1)) + nt(dv, cols(w3, 2))).astype(BF)
    dx, dg2, db2 = norm_bwd(mid, gains[2], nt(dq, cols(w3, 0)))
    small = jnp.stack([dg1, dg2, db1, db2])
    return decoded.astype(BF), d_joined + dx, d_mem, grad2, grad3, small


def on_device(layer_in, segment_ids, out_grads, w_qkv, w_out, w_up, w_down, norm_gain, norm_bias, w_qc, w_kvc, w_oc):
    encoder = lax.axis_index("section") == 0
    core = lax.axis_index("dp") & 1
    place = lax.axis_index("mp")
    ways = lax.axis_size("mp")
    rows = layer_in.shape[1]
    width = layer_in.shape[3]
    blk = w_qkv.shape[1]

    shard1 = jnp.concatenate([w_qkv[0].reshape(blk, -1), w_out[0].T], axis=1)
    shard2 = jnp.concatenate([w_up[0], w_down[0].T], axis=1)
    mine3 = jnp.stack([w_qc, w_kvc[:, 0], w_kvc[:, 1], w_oc.T], axis=1)
    theirs3 = swap(mine3, "section", 1)
    shard3 = jnp.where(
        encoder,
        jnp.concatenate([mine3, theirs3], axis=2),
        jnp.concatenate([theirs3, mine3], axis=2),
    ).reshape(blk, -1)
    own = rows_in(layer_in[0], core)
    w1 = assemble(gather_blocks(shard1))
    norms = jnp.concatenate([norm_gain[0], norm_bias[0]])
    norms = lax.all_gather(norms, ("dp", "mp"), axis=1, tiled=True)
    gains, biases = norms[:3], norms[3:]
    w2 = assemble(gather_blocks(shard2))
    w3 = assemble(gather_blocks(shard3))
    cots = rows_in(out_grads[0], core).astype(F32)

    other_segs = swap(segment_ids, "dp", 1)
    segs = jnp.where(
        core == 0,
        jnp.concatenate([segment_ids, other_segs], axis=1),
        jnp.concatenate([other_segs, segment_ids], axis=1),
    )
    segs = lax.dynamic_index_in_dim(segs, place, axis=1, keepdims=False)
    segs = segs.reshape(2, ways, 2, -1)
    even, odd = segs[:, :, 0].reshape(2, -1), segs[:, :, 1].reshape(2, -1)
    segs = jnp.where(
        core == 0, jnp.concatenate([even, odd], axis=1), jnp.concatenate([odd, even], axis=1)
    )
    half = segs.shape[1] // 2
    seg_own = jnp.where(encoder, segs[0], segs[1])

    x_full = jnp.concatenate([own, swap(own, "dp", 1)])
    normed, q, k, v, att, lse, mid = self_fwd(x_full, seg_own, w1, gains[0], biases[0])

    def encode(_):
        out, hidden, slope = feed_fwd(mid, w2, gains[1], biases[1])
        return out, norm_fwd(out, gains[2], biases[2]), hidden, slope

    wide = (half, shard2.shape[1] // 2 * ways)

    def skip(_):
        return (
            jnp.zeros((half, width), F32),
            jnp.zeros((half, width), BF),
            jnp.zeros(wide, BF),
            jnp.zeros(wide, BF),
        )

    encoded, memory, hidden, slope = lax.cond(encoder, encode, skip, 0)
    mem_own = oneway(memory, "section", 0, 1)
    mem_full = jnp.concatenate([mem_own, swap(mem_own, "dp", 1)])

    def decode(_):
        return cross_both(mid, mem_full, cots, segs[1, :half], segs[0], w2, w3, gains, biases)

    def skip2(_):
        return jax.tree.map(
            lambda s: jnp.zeros(s.shape, s.dtype), jax.eval_shape(decode, 0)
        )

    decoded, d_mid, d_mem, grad2, grad3, small = lax.cond(encoder, skip2, decode, 0)
    section_out = rows_out(jnp.where(encoder, memory, decoded), core, rows)[None]
    d_mem = (d_mem[:half].astype(F32) + swap(d_mem[half:], "dp", 1).astype(F32)).astype(BF)
    d_mem = oneway(d_mem, "section", 1, 0)

    def encode_back(_):
        d_out, dg2, db2 = norm_bwd(encoded, gains[2], d_mem.astype(F32) + cots)
        d, g2, dg1, db1 = feed_bwd(mid, d_out, hidden, slope, w2, gains[1], biases[1])
        return d, g2, jnp.stack([dg1, dg2, db1, db2])

    d_mid, grad2, small = lax.cond(encoder, encode_back, lambda _: (d_mid, grad2, small), 0)
    d_own, d_other, grad1 = self_bwd(d_mid, normed, q, k, v, att, lse, seg_own, w1)
    d_own = d_own + swap(d_other, "dp", 1).astype(F32)
    dx, dg0, db0 = norm_bwd(own.astype(F32), gains[0], d_own)
    in_grads = rows_out((d_mid + dx).astype(BF), core, rows)[None]

    r2 = reduce_blocks(to_relative(grad2))
    r3 = reduce_blocks(to_relative(grad3))
    r1 = reduce_blocks(to_relative(grad1))
    grad_qkv = r1[:, :384].reshape(1, blk, 3, -1)
    grad_out = r1[:, 384:].T[None]
    span = r2.shape[1] // 2
    grad_up = r2[None, :, :span]
    grad_down = r2[:, span:].T[None]
    r3 = r3.reshape(blk, 4, 2, -1)
    back = oneway(r3[:, :, 0].astype(BF), "section", 1, 0).astype(F32)
    r3 = jnp.where(encoder, back, r3[:, :, 1])
    grad_qc, grad_kvc, grad_oc = r3[:, 0], r3[:, 1:3], r3[:, 3].T
    small = jnp.concatenate([dg0[None], small[:2], db0[None], small[2:]])
    small = lax.psum_scatter(small, ("dp", "mp"), scatter_dimension=1, tiled=True)
    grad_gain = small[None, :3]
    grad_bias = jnp.stack([small[3], small[5]])[None]
    grad_ffn = small[4][None]
    return (
        section_out,
        in_grads,
        grad_qkv,
        grad_out,
        grad_up,
        grad_down,
        grad_gain,
        grad_bias,
        grad_ffn,
        grad_qc,
        grad_kvc,
        grad_oc,
    )


def solution(mesh):
    placed = (
        P("section", "dp", "mp", None),
        P(None, "dp", None),
        P("section", "dp", "mp", None),
        P("section", "dp", None, "mp"),
        P("section", "mp", "dp"),
        P("section", "dp", "mp"),
        P("section", "mp", "dp"),
        P("section", None, ("dp", "mp")),
        P("section", None, ("dp", "mp")),
        P("dp", ("section", "mp")),
        P("dp", None, ("section", "mp")),
        P(("section", "mp"), "dp"),
    )
    return jax.shard_map(
        on_device,
        mesh=mesh,
        in_specs=placed,
        out_specs=(
            P("section", "dp", "mp", None),
            P("section", "dp", "mp", None),
            P("section", "dp", None, "mp"),
            P("section", "mp", "dp"),
            P("section", "dp", "mp"),
            P("section", "mp", "dp"),
            P("section", None, ("dp", "mp")),
            P("section", None, ("dp", "mp")),
            P("section", ("dp", "mp")),
            P("dp", ("section", "mp")),
            P("dp", None, ("section", "mp")),
            P(("section", "mp"), "dp"),
        ),
        check_vma=False,
    )
```

```python
import functools

import jax
import jax.numpy as jnp
from jax import lax
from jax.experimental import pallas as pl
from jax.experimental.pallas import tpu as pltpu
from jax.sharding import PartitionSpec as P

HD = 64
PAIR = 2 * HD
EPS = 1e-05
BIG = 1e30
FACTOR = HD**-0.5
LOG2E = 1.4426950408889634
BF = jnp.bfloat16
F32 = jnp.float32
PAD = 16
VMEM_LIMIT = 56 * 1024 * 1024


def swap(block, axis, bit):
    count = lax.axis_size(axis)
    return lax.ppermute(block, axis, [(i, i ^ bit) for i in range(count)])


def oneway(block, axis, source, target):
    return lax.ppermute(block, axis, [(source, target)])


def dp_bits():
    count = lax.axis_size("dp")
    return [1 << b for b in range(1, count.bit_length() - 1)]


def relative_order():
    order = [0]
    for bit in dp_bits():
        order = order + [a ^ bit for a in order]
    return order + [a ^ 1 for a in order]


def after(x, *others):
    return lax.optimization_barrier((x, others))[0]


def decoder_swap(block, axis, bit):
    count = lax.axis_size(axis)
    pairs = [(count + i, count + (i ^ bit)) for i in range(count)]
    return lax.ppermute(block, ("section", axis), pairs)


def doubled(arrays, bits, move=swap):
    for bit in bits:
        arrays = arrays + [(move(x, "dp", bit), a ^ bit) for x, a in arrays]
    return arrays


def add(a, b):
    return (a.astype(F32) + b.astype(F32)).astype(BF)


def fold(keep, got):
    half = keep.shape[0] // 2
    return add(keep[:half], got[:half]), add(keep[half:], got[half:])


def fold_dp(keep, got, move=swap):
    for bit in dp_bits()[::-1]:
        keep, send = fold(keep, got)
        got = move(send, "dp", bit)
    return keep[0], got[0]


def fold_mp(keep, got, turns, move=swap):
    total = None
    for n, b in enumerate(turns):
        if b:
            part = move(add(keep[n], got[n]), "mp", b).astype(F32)
        else:
            part = keep[n].astype(F32) + got[n].astype(F32)
        total = part if total is None else total + part
    return total


def row_route(turn, back):
    ways = lax.axis_size("mp")
    route = []
    for dp in range(lax.axis_size("dp")):
        for place in range(ways):
            e = place ^ turn
            target = ((dp & ~1) | (e >> 1)) * ways + 2 * (dp & 1) + (e & 1)
            route.append((target, dp * ways + place) if back else (dp * ways + place, target))
    return route


def rows_in(local):
    place = lax.axis_index("mp")
    span = local.shape[1] // 2
    pieces = []
    for turn in range(4):
        e = place ^ turn
        piece = lax.dynamic_slice(local, (e & 1, (e >> 1) * span, 0), (1, span, local.shape[2]))
        pieces.append(lax.ppermute(piece[0], ("dp", "mp"), row_route(turn, False)))
    return jnp.concatenate(pieces)


def xor_order(x, me):
    count = x.shape[0]
    bit = 1
    while bit < count:
        flipped = x.reshape((count // (2 * bit), 2, bit) + x.shape[1:])[:, ::-1].reshape(x.shape)
        x = jnp.where((me & bit) > 0, flipped, x)
        bit *= 2
    return x


def rows_out(own):
    span = own.shape[0] // 4
    pieces = [
        lax.ppermute(own[t * span : (t + 1) * span], ("dp", "mp"), row_route(t, True))
        for t in range(4)
    ]
    tiles = xor_order(jnp.stack(pieces), lax.axis_index("mp"))
    return tiles.reshape(2, 2, span, -1).transpose(1, 0, 2, 3).reshape(2, 2 * span, -1)


def mm(a, b):
    return jnp.dot(a, b, preferred_element_type=F32)


def nt(a, b):
    return lax.dot_general(a, b, (((1,), (1,)), ((), ())), preferred_element_type=F32)


def stats(states):
    average = jnp.mean(states, axis=-1, keepdims=True)
    centred = states - average
    inv = lax.rsqrt(jnp.mean(centred * centred, axis=-1, keepdims=True) + EPS)
    return centred * inv, inv


def norm_fwd(states, gain, bias):
    hat, _ = stats(states)
    return (hat * gain + bias).astype(BF)


def norm_bwd(states, gain, grad):
    hat, inv = stats(states)
    e = grad * gain
    dx = inv * (
        e - jnp.mean(e, axis=-1, keepdims=True) - hat * jnp.mean(e * hat, axis=-1, keepdims=True)
    )
    return dx, jnp.sum(grad * hat, axis=0, keepdims=True), jnp.sum(grad, axis=0, keepdims=True)


def gelu_parts(pre):
    size = jnp.abs(pre)
    bell = jnp.exp2(pre * pre * (-0.5 * LOG2E))
    t = 1.0 / (1.0 + (0.3275911 * 0.5**0.5) * size)
    poly = 1.061405429 * t - 1.453152027
    poly = poly * t + 1.421413741
    poly = poly * t - 0.284496736
    poly = poly * t + 0.254829592
    tail = 0.5 * poly * t * bell
    return jnp.where(pre >= 0, 1.0 - tail, tail), 0.3989422804014327 * bell


def lanes(rows):
    return lax.broadcasted_iota(jnp.int32, (rows, PAIR), 1)


def head_part(h, real, other):
    lane = lanes(real.shape[0])
    mine = (lane >= HD) if h else (lane < HD)
    return jnp.where(mine, real.astype(F32), other).astype(BF)


def query_code(code):
    return code.astype(F32)


def key_code(code):
    lane = lanes(code.shape[0])
    return jnp.where((lane & (HD - 1)) < 4, (code.astype(F32) - 1.0) * BIG, 0.0)


def start(copies):
    for copy in copies:
        copy.start()
    return copies


def wait(copies):
    for copy in copies:
        copy.wait()


def moves(pairs, sems):
    return [pltpu.make_async_copy(a, b, sems.at[n]) for n, (a, b) in enumerate(pairs)]


def load_weights(me, refs, pieces, target, sems):
    count = sum(1 for piece in pieces if piece[2] == 0)
    blk = target.shape[1] // count
    copies = []
    for n, (ref, lead, first, pairs, a) in enumerate(pieces):
        rows = pl.ds(pl.multiple_of((me ^ a) * blk, blk), blk)
        if pairs is None:
            source, place = refs[ref].at[lead + (pl.ds(0, blk),)], target.at[first, rows]
        else:
            source = refs[ref].at[lead + (pl.ds(0, pairs), pl.ds(0, blk))]
            place = target.at[pl.ds(first, pairs), rows]
        copies.append(pltpu.make_async_copy(source, place, sems.at[n]))
    return start(copies)


def kernel_order(count):
    order = [0]
    bit = 2
    while bit < count:
        order = order + [a ^ bit for a in order]
        bit *= 2
    return order + [a ^ 1 for a in order]


def store_grad(me, staged, b, keep, send, sems):
    count = 2 * keep.shape[0]
    blk = staged.shape[1] // count
    copies = []
    for n, a in enumerate(kernel_order(count)):
        target = keep.at[n] if n < count // 2 else send.at[n - count // 2]
        rows = pl.ds(pl.multiple_of((me ^ a) * blk, blk), blk)
        copies.append(
            pltpu.make_async_copy(staged.at[b, rows, :], target.at[b], sems.at[b, n])
        )
    return copies


def attend_pair(q, k, v, code_q, code_k, b, logs):
    rows = q.shape[0]
    wide_v = jnp.concatenate([v, jnp.ones_like(v)], axis=1)
    scale = FACTOR * LOG2E
    outs = []
    for h in range(2):
        qa = head_part(h, q, query_code(code_q))
        ka = head_part(h, k, key_code(code_k))
        s = nt(qa, ka)
        top = jnp.max(s, axis=1, keepdims=True)
        p = jnp.exp2((s - top) * scale).astype(BF)
        o = mm(p, wide_v)
        total = o[:, PAIR:]
        outs.append(o[:, :PAIR] / total)
        logs[...] = jnp.where(lanes(rows) == 2 * b + h, top * scale + jnp.log2(total), logs[...])
    return jnp.where(lanes(rows) < HD, outs[0], outs[1])


def attend_pair_back(q, k, v, att, do, code_q, code_k, logs_ref, b):
    rows = q.shape[0]
    scale = FACTOR * LOG2E
    k_t = k.T
    prod = do.astype(F32) * att
    high = prod.astype(BF)
    low = (prod - high.astype(F32)).astype(BF)
    row = lax.broadcasted_iota(jnp.int32, (8, PAIR), 0)
    lane = lax.broadcasted_iota(jnp.int32, (8, PAIR), 1)
    pick = jnp.where((lane // HD) == row, 1.0, 0.0).astype(BF)
    delta = nt(pick, high) + nt(pick, low)
    dk = dv = 0.0
    dq_t = []
    for h in range(2):
        qa = head_part(h, q, query_code(code_q))
        ka = head_part(h, k, key_code(code_k))
        qm = head_part(h, q, 0.0)
        dm = head_part(h, do, 0.0)
        log = logs_ref[pl.ds(2 * b + h, 1), :]
        p_t = jnp.exp2(nt(ka, qa) * scale - log)
        ds_t = (p_t * (nt(v, dm) - delta[h : h + 1])).astype(BF)
        dv = dv + mm(p_t.astype(BF), dm)
        dk = dk + mm(ds_t, qm)
        dq_t.append(mm(k_t, ds_t))
    sub = lax.broadcasted_iota(jnp.int32, (PAIR, rows), 0)
    dq = jnp.where(sub < HD, dq_t[0], dq_t[1]).T
    return (dq * FACTOR).astype(BF), (dk * FACTOR).astype(BF), dv.astype(BF)


def columns(wbuf, pairs, at):
    return jnp.concatenate([wbuf[b, :, at * PAIR : (at + 1) * PAIR] for b in pairs], axis=1)


def lane_pairs(x, count):
    return [x[:, n * PAIR : (n + 1) * PAIR] for n in range(count)]


def attention_fwd(pairs, q_src, kv_src, code_q, code_k, wbuf, q_buf, k_buf, v_buf, att_buf, logs, total, emit):
    count = len(pairs)
    logs[...] = jnp.zeros_like(logs)
    queries = mm(q_src[...], columns(wbuf, pairs, 0)).astype(BF)
    for n, q in enumerate(lane_pairs(queries, count)):
        q_buf[n] = q
    for n, b in enumerate(pairs):
        kv = mm(kv_src[...], wbuf[b, :, PAIR : 3 * PAIR]).astype(BF)
        k_buf[n] = kv[:, :PAIR]
        v_buf[n] = kv[:, PAIR:]
        att_buf[n] = attend_pair(
            q_buf[n], k_buf[n], v_buf[n], code_q[...], code_k[...], n, logs
        )
        emit(n)
    attended = jnp.concatenate([att_buf[n].astype(BF) for n in range(count)], axis=1)
    total[...] += nt(attended, columns(wbuf, pairs, 3))


def attention_bwd(me, pairs, low, low_t, q_src_t, kv_src_t, code_q, code_k, wbuf, q_buf, k_buf, v_buf, att_buf, logs, do_buf, d_q_src, d_kv_src, staged, keep, send, gsems):
    count = len(pairs)
    for n, do in enumerate(lane_pairs(mm(low[...], columns(wbuf, pairs, 3)).astype(BF), count)):
        do_buf[n] = do
    attended = jnp.concatenate([att_buf[n].astype(BF) for n in range(count)], axis=1)
    for n, part in enumerate(lane_pairs(mm(low_t[...], attended).astype(BF), count)):
        staged[n, :, 3 * PAIR :] = part
    dqs = []
    for n, b in enumerate(pairs):
        dq, dk, dv = attend_pair_back(
            q_buf[n], k_buf[n], v_buf[n], att_buf[n], do_buf[n], code_q[...], code_k[...], logs, n
        )
        dqs.append(dq)
        dkv = jnp.concatenate([dk, dv], axis=1)
        staged[n, :, PAIR : 3 * PAIR] = mm(kv_src_t[...], dkv).astype(BF)
        part = nt(dkv, wbuf[b, :, PAIR : 3 * PAIR])
        d_kv_src[...] = part if n == 0 else d_kv_src[...] + part
    dq = jnp.concatenate(dqs, axis=1)
    for n, part in enumerate(lane_pairs(mm(q_src_t[...], dq).astype(BF), count)):
        staged[n, :, :PAIR] = part
    copies = []
    for n in range(count):
        copies += start(store_grad(me, staged, n, keep, send, gsems))
    d_q_src[...] = nt(dq, columns(wbuf, pairs, 0))
    return copies


def self_fwd_kernel(pieces, n_weights, pairs, ints, x_own, x_other, code_in, norms, *refs):
    first = pairs[0] == 0
    weights, refs = refs[:n_weights], refs[n_weights:]
    if first:
        q_ref, k_ref, v_ref, att_ref, logs_ref, mid_ref, normed_ref = refs[:7]
        mid_in = normed_in = None
        refs = refs[7:]
    else:
        mid_in, normed_in, q_ref, k_ref, v_ref, att_ref, logs_ref, mid_ref, normed_ref = refs[:9]
        refs = refs[9:]
    wbuf, own, other, code, normed, mid, q_buf, k_buf, v_buf, att_buf, logs, logs_t, turned, wsems, sems, osems = refs
    me = ints[0]
    half = own.shape[0]
    weight_copies = load_weights(me, weights, pieces, wbuf, wsems)
    if first:
        loads = start(moves([(x_own, own), (x_other, other), (code_in, code)], sems))
        wait(loads[:2])
        states = own[...].astype(F32)
        mid[...] = states
        normed[:half] = norm_fwd(states, norms[0:1], norms[3:4])
        normed[half:] = norm_fwd(other[...].astype(F32), norms[0:1], norms[3:4])
    else:
        loads = start(moves([(mid_in, mid), (normed_in, normed), (code_in, code)], sems))
        wait(loads[:2])
    wait(loads[2:])
    wait(weight_copies)
    outs = []

    def emit(n):
        sources = [(q_buf, q_ref), (k_buf, k_ref), (v_buf, v_ref), (att_buf, att_ref)]
        outs.extend(start(moves([(a.at[n], b.at[n]) for a, b in sources], osems.at[n])))

    attention_fwd(
        pairs, normed.at[:half], normed, code.at[:half], code, wbuf, q_buf, k_buf, v_buf, att_buf, logs, mid, emit
    )
    last = [(mid, mid_ref), (logs_t, logs_ref), (normed, normed_ref)]
    if not first:
        turned[...] = normed[...].T
        last[2] = (turned, normed_ref)
    logs_t[...] = logs[...].T[: logs_t.shape[0]]
    outs.extend(start(moves(last, osems.at[len(pairs)])))
    wait(outs)


def self_bwd_kernel(pieces, n_weights, pairs, ints, d_mid_in, code_in, q_in, k_in, v_in, att_in, logs_in, normed_t_in, *refs):
    weights, refs = refs[:n_weights], refs[n_weights:]
    d_own_ref, d_other_ref, keep, send = refs[:4]
    wbuf, d_mid, code, q_buf, k_buf, v_buf, att_buf, logs, normed_t, low, low_t, do_buf, d_q, d_kv, d_other, staged, wsems, sems, gsems = refs[4:]
    me = ints[0]
    half = d_mid.shape[0]
    loads = start(
        moves(
            [(d_mid_in, d_mid), (code_in, code), (q_in, q_buf), (k_in, k_buf), (v_in, v_buf), (att_in, att_buf), (logs_in, logs), (normed_t_in, normed_t)],
            sems,
        )
    )
    weight_copies = load_weights(me, weights, pieces, wbuf, wsems)
    wait(loads[:1])
    low[...] = d_mid[...].astype(BF)
    low_t[...] = low[...].T
    wait(loads[1:])
    wait(weight_copies)
    copies = attention_bwd(
        me, pairs, low, low_t, normed_t.at[:, :half], normed_t, code.at[:half], code, wbuf, q_buf, k_buf, v_buf, att_buf, logs, do_buf, d_q, d_kv, staged, keep, send, gsems
    )
    d_other[...] = d_kv[half:].astype(BF)
    outs = start(moves([(d_other, d_other_ref)], sems.at[pl.ds(0, 1)]))
    d_q[...] += d_kv[:half]
    outs += start(moves([(d_q, d_own_ref)], sems.at[pl.ds(1, 1)]))
    wait(outs + copies)


def feed_fwd_kernel(pieces, n_weights, ints, mid_in, norms, *refs):
    weights, refs = refs[:n_weights], refs[n_weights:]
    out_ref, memory_ref, hidden_ref, slope_ref = refs[:4]
    up, down, mid, out, memory, hidden_buf, slope_buf, normed, wsems, sems, osems = refs[4:]
    me = ints[0]

    @pl.when(ints[1] == 1)
    def _():
        loads = start(moves([(mid_in, mid)], sems))
        ups = load_weights(me, weights, pieces[0], up, wsems.at[0])
        downs = load_weights(me, weights, pieces[1], down, wsems.at[1])
        wait(loads)
        normed[...] = norm_fwd(mid[...], norms[1:2], norms[4:5])
        wait(ups)
        wait(downs)
        outs = []
        for b in range(up.shape[0]):
            pre = mm(normed[...], up[b])
            cdf, density = gelu_parts(pre)
            hidden_buf[b] = (pre * cdf).astype(BF)
            slope_buf[b] = (cdf + pre * density).astype(BF)
            base = mid[...] if b == 0 else out[...]
            out[...] = base + nt(hidden_buf[b], down[b])
            outs += start(
                moves([(hidden_buf.at[b], hidden_ref.at[b]), (slope_buf.at[b], slope_ref.at[b])], osems.at[b])
            )
        outs += start(moves([(out, out_ref)], osems.at[up.shape[0]]))
        memory[...] = norm_fwd(out[...], norms[2:3], norms[5:6])
        outs += start(moves([(memory, memory_ref)], sems))
        wait(outs)


def decoder_kernel(pieces, n_weights, ints, mid_in, mem_own, mem_other, code_q_in, code_k_in, cots_in, norms, *refs):
    weights, refs = refs[:n_weights], refs[n_weights:]
    decoded_ref, d_mid_ref, mem_keep, mem_send, small, keep2, send2, keep3, send3 = refs[:9]
    (
        wbuf, up, down, mid, mem, code_q, code_k, cots, cross_in, q_buf, k_buf, v_buf, att_buf, logs, logs_t,
        joined, out, decoded, normed, normed_t, low, low_t, mem_t, do_buf, d_norm, d_q, d_kv, d_mem,
        staged2, staged3, wsems, sems, osems, gsems2, gsems3,
    ) = refs[9:]
    me = ints[0]
    half = mid.shape[0]

    @pl.when(ints[1] == 0)
    def _():
        loads = start(
            moves(
                [(mid_in, mid), (mem_own, mem.at[:half]), (mem_other, mem.at[half:]), (code_q_in, code_q), (code_k_in, code_k), (cots_in, cots)],
                sems,
            )
        )
        crosses = load_weights(me, weights, pieces[0], wbuf, wsems.at[0])
        ups = load_weights(me, weights, pieces[1], up, wsems.at[1])
        downs = load_weights(me, weights, pieces[2], down, wsems.at[2])
        pairs = list(range(wbuf.shape[0]))
        wait(loads[:1])
        joined[...] = mid[...]
        cross_in[...] = norm_fwd(mid[...], norms[2:3], norms[5:6])
        wait(loads[1:])
        wait(crosses)
        attention_fwd(
            pairs, cross_in, mem, code_q, code_k, wbuf, q_buf, k_buf, v_buf, att_buf, logs, joined, lambda n: None
        )
        logs_t[...] = logs[...].T[: logs_t.shape[0]]
        wait(ups)
        wait(downs)
        normed[...] = norm_fwd(joined[...], norms[1:2], norms[4:5])
        normed_t[...] = normed[...].T
        low_t[...] = cots[...].T
        unit = up.shape[2]
        copies = []
        for b in pairs:
            pre = mm(normed[...], up[b])
            cdf, density = gelu_parts(pre)
            hidden = (pre * cdf).astype(BF)
            base = joined[...] if b == 0 else out[...]
            out[...] = base + nt(hidden, down[b])
            d_pre = (mm(cots[...], down[b]) * (cdf + pre * density)).astype(BF)
            staged2[b, :, :unit] = mm(normed_t[...], d_pre).astype(BF)
            staged2[b, :, unit:] = mm(low_t[...], hidden).astype(BF)
            copies += start(store_grad(me, staged2, b, keep2, send2, gsems2))
            part = nt(d_pre, up[b])
            d_norm[...] = part if b == 0 else d_norm[...] + part
        decoded[...] = out[...].astype(BF)
        outs = start(moves([(decoded, decoded_ref)], osems))
        dx, d_gain1, d_bias1 = norm_bwd(joined[...], norms[1:2], d_norm[...])
        joined[...] = cots[...].astype(F32) + dx
        low[...] = joined[...].astype(BF)
        low_t[...] = low[...].T
        mem_t[...] = mem[...].T
        normed_t[...] = cross_in[...].T
        copies += attention_bwd(
            me, pairs, low, low_t, normed_t, mem_t, code_q, code_k, wbuf, q_buf, k_buf, v_buf, att_buf, logs_t, do_buf, d_q, d_kv, staged3, keep3, send3, gsems3
        )
        d_mem[...] = d_kv[...].astype(BF)
        outs += start(
            moves([(d_mem.at[half:], mem_send), (d_mem.at[:half], mem_keep)], osems.at[pl.ds(1, 2)])
        )
        dx, d_gain2, d_bias2 = norm_bwd(mid[...], norms[2:3], d_q[...])
        out[...] = joined[...] + dx
        outs += start(moves([(out, d_mid_ref)], osems.at[pl.ds(3, 1)]))
        small[0:1] = d_gain1
        small[1:2] = d_gain2
        small[2:3] = d_bias1
        small[3:4] = d_bias2
        wait(outs + copies)


def feed_bwd_kernel(pieces, n_weights, ints, encoded_in, mid_in, d_mem_in, cots_in, norms, hidden_in, slope_in, small_in, d_mid_in, keep_in, send_in, *refs):
    weights, refs = refs[:n_weights], refs[n_weights:]
    small, d_mid_ref, keep, send = refs[:4]
    (
        up, down, encoded, mid, d_mem, cots, hidden, slope, normed_t, low, low_t, d_out, d_norm, staged, wsems, sems, gsems,
    ) = refs[4:]
    me = ints[0]

    @pl.when(ints[1] == 0)
    def _():
        small[...] = small_in[...]

    @pl.when(ints[1] == 1)
    def _():
        loads = start(
            moves(
                [(encoded_in, encoded), (d_mem_in, d_mem), (cots_in, cots), (mid_in, mid), (hidden_in, hidden), (slope_in, slope)],
                sems,
            )
        )
        downs = load_weights(me, weights, pieces[1], down, wsems.at[1])
        ups = load_weights(me, weights, pieces[0], up, wsems.at[0])
        wait(loads[:3])
        grad = d_mem[...].astype(F32) + cots[...].astype(F32)
        dx, d_gain, d_bias = norm_bwd(encoded[...], norms[2:3], grad)
        small[1:2] = d_gain
        small[3:4] = d_bias
        d_out[...] = dx
        low[...] = dx.astype(BF)
        low_t[...] = low[...].T
        wait(loads[3:])
        normed_t[...] = norm_fwd(mid[...], norms[1:2], norms[4:5]).T
        wait(downs)
        wait(ups)
        ways, _, unit = up.shape
        copies = []
        for b in range(ways):
            d_pre = (mm(low[...], down[b]) * slope[b].astype(F32)).astype(BF)
            staged[b, :, :unit] = mm(normed_t[...], d_pre).astype(BF)
            staged[b, :, unit:] = mm(low_t[...], hidden[b]).astype(BF)
            copies += start(store_grad(me, staged, b, keep, send, gsems))
            part = nt(d_pre, up[b])
            d_norm[...] = part if b == 0 else d_norm[...] + part
        dx, d_gain1, d_bias1 = norm_bwd(mid[...], norms[1:2], d_norm[...])
        d_out[...] += dx
        outs = start(moves([(d_out, d_mid_ref)], sems))
        small[0:1] = d_gain1
        small[2:3] = d_bias1
        wait(outs + copies)


def last_kernel(d_own1, d_own2, d_got1, d_got2, x_own, d_mid, norms, dx_ref, small):
    grad = d_own1[...] + d_own2[...] + d_got1[...].astype(F32) + d_got2[...].astype(F32)
    dx, d_gain, d_bias = norm_bwd(x_own[...].astype(F32), norms[0:1], grad)
    dx_ref[...] = (d_mid[...] + dx).astype(BF)
    small[0:1] = d_gain
    small[1:2] = d_bias


VM = pl.BlockSpec(memory_space=pltpu.VMEM)
SM = pl.BlockSpec(memory_space=pltpu.SMEM)
AN = pl.BlockSpec(memory_space=pl.ANY)


def call(kernel, name, ins, outs, scratch, flops, **more):
    return pl.pallas_call(
        kernel,
        name=name,
        in_specs=[spec for _, spec in ins],
        out_shape=[jax.ShapeDtypeStruct(shape, dtype) for shape, dtype, _ in outs],
        out_specs=[spec for _, _, spec in outs],
        scratch_shapes=scratch,
        compiler_params=pltpu.CompilerParams(vmem_limit_bytes=VMEM_LIMIT),
        cost_estimate=pl.CostEstimate(flops=flops, bytes_accessed=8 << 20, transcendentals=0),
        **more,
    )(*[array for array, _ in ins])


def on_device(layer_in, segment_ids, out_grads, w_qkv, w_out, w_up, w_down, norm_gain, norm_bias, w_qc, w_kvc, w_oc):
    encoder = lax.axis_index("section") == 0
    me = lax.axis_index("dp")
    core = me & 1
    place = lax.axis_index("mp")
    ways = lax.axis_size("mp")
    count = lax.axis_size("dp")
    rows = layer_in.shape[1]
    width = layer_in.shape[3]
    blk = w_qkv.shape[1]
    half = 2 * layer_in.shape[2]
    length = 2 * half
    assert rows == 2 and ways == 4 and length == segment_ids.shape[2]
    ints = jnp.stack([me, encoder.astype(jnp.int32)])

    norms = jnp.concatenate([norm_gain[0], norm_bias[0]]).reshape(1, -1)
    high = norms.astype(BF)
    low = (norms - high.astype(F32)).astype(BF)
    line = jnp.concatenate([high, low], axis=1)
    shard1 = jnp.concatenate([w_qkv[0].reshape(blk, -1), w_out[0].T], axis=1)
    line = jnp.pad(line, ((0, PAD - 1), (0, shard1.shape[1] - line.shape[1])))
    shard1 = jnp.concatenate([shard1, line])
    shard2 = jnp.concatenate([w_up[0], w_down[0].T], axis=1)
    mine3 = jnp.stack([w_qc, w_kvc[:, 0], w_kvc[:, 1], w_oc.T], axis=1)
    theirs3 = swap(mine3, "section", 1)
    shard3 = jnp.where(
        encoder,
        jnp.concatenate([mine3, theirs3], axis=2),
        jnp.concatenate([theirs3, mine3], axis=2),
    ).reshape(blk, -1)

    up_shard, down_shard = w_up[0], w_down[0].T
    bits, core_bit = dp_bits(), [1]
    others = range(1, ways)
    first1 = jnp.stack([shard1] + [swap(shard1, "mp", b) for b in others])
    x_own = rows_in(layer_in[0])
    slots = jnp.stack(
        [jnp.where(encoder, up_shard, shard3), jnp.where(encoder, down_shard, up_shard), down_shard]
    )
    own_slots = doubled(doubled([(slots, 0)], bits), core_bit)
    w1 = doubled(doubled([(first1, 0)], bits), core_bit)
    x_other = swap(x_own, "dp", 1)
    slots = after(slots, x_own)
    z_a = [swap(slots[0], "mp", b) for b in others]
    z_b = [swap(slots[1], "mp", b) for b in others]

    each = norms.shape[1] // 6
    lines = jnp.stack([w[:, blk, : 12 * each] for w, _ in w1])
    order = relative_order()
    lines = jnp.stack([lines[order.index(a)] for a in range(count)])
    lines = xor_order(lines, me)
    lines = xor_order(lines.swapaxes(0, 1), place).swapaxes(0, 1)
    lines = lines.reshape(count, ways, 2, 6, each).astype(F32)
    norms = (lines[:, :, 0] + lines[:, :, 1]).transpose(2, 0, 1, 3).reshape(6, width)
    norms = jnp.pad(norms, ((0, 2), (0, 0)))

    other_segs = swap(segment_ids, "dp", 1)
    segs = jnp.where(core == (place >> 1), segment_ids, other_segs)
    segs = jnp.where((place & 1) == 0, segs[:, 0], segs[:, 1])
    segs = segs.reshape(2, ways, 2, -1).transpose(1, 2, 0, 3)
    segs = xor_order(segs, (core << 1) | (place & 1))
    segs = jnp.where(core == 0, segs, segs[:, ::-1])
    mine, theirs = segs[:, 0], segs[:, 1]
    theirs = theirs.reshape((2, 2) + theirs.shape[1:])[::-1].reshape(theirs.shape)
    segs = jnp.concatenate([mine, theirs]).transpose(1, 0, 2).reshape(2, length)
    lane = jnp.arange(PAIR) & (HD - 1)
    codes = (segs[:, :, None] == lane[None, None, :]).astype(BF)
    code_own = jnp.where(encoder, codes[0], codes[1])

    unit = up_shard.shape[1]
    middle = ways // 2
    halves = (list(range(middle)), list(range(middle, ways)))
    dma = pltpu.SemaphoreType.DMA

    def buf(*shape):
        return pltpu.VMEM(shape, BF)

    def fbuf(*shape):
        return pltpu.VMEM(shape, F32)

    def hbm(*arrays):
        return [(a, AN) for a in arrays]

    wbuf = buf(ways, width, 4 * PAIR)
    pieces1 = [(n, (), 0, ways, a) for n, (_, a) in enumerate(w1)]
    weights1 = [w for w, _ in w1]

    def kept(count):
        return [
            ((count, half, PAIR), BF, AN),
            ((count, length, PAIR), BF, AN),
            ((count, length, PAIR), BF, AN),
            ((count, half, PAIR), F32, AN),
            ((8, half), F32, AN),
        ]

    def kept_bufs(count):
        return [buf(count, half, PAIR), buf(count, length, PAIR), buf(count, length, PAIR), fbuf(count, half, PAIR)]

    def grads(pairs, columns):
        return [((count // 2, pairs, blk, columns), BF, AN)] * 2

    state, state_low = ((half, width), F32, AN), ((half, width), BF, AN)

    def self_fwd(pairs, more):
        turned = (width, length) if pairs[0] else (length, width)
        return call(
            functools.partial(self_fwd_kernel, pieces1, len(weights1), pairs),
            "self_fwd",
            [(ints, SM)] + hbm(x_own, x_other, code_own) + [(norms, VM)] + hbm(*weights1, *more),
            kept(len(pairs)) + [state, (turned, BF, AN)],
            [wbuf, buf(half, width), buf(half, width), buf(length, PAIR), buf(length, width), fbuf(half, width)]
            + kept_bufs(len(pairs))
            + [fbuf(half, PAIR), fbuf(8, half), buf(width, length), dma((count,)), dma((3,)), dma((len(pairs) + 1, 4))],
            5 << 30,
        )

    *kept_a, mid, normed = self_fwd(halves[0], ())
    z_a = after(z_a, mid)
    rest_a = doubled([(jnp.stack(z_a), 0)], bits)
    *kept_b, mid, normed_t = self_fwd(halves[1], (mid, normed))
    z_b = after(z_b, mid)
    rest_b = doubled([(jnp.stack(z_b), 0)], bits)
    z_c = [decoder_swap(after(slots[2], mid), "mp", b) for b in others]
    rest_a = doubled(rest_a, core_bit)
    rest_b = doubled(rest_b, core_bit)
    cots = rows_in(after(out_grads[0], mid))

    def slot(arrays, at, rest):
        base = len(arrays)
        arrays.extend(x for x, _ in own_slots)
        arrays.extend(x for x, _ in rest)
        found = [(base + n, (at,), 0, None, a) for n, (_, a) in enumerate(own_slots)]
        base += len(own_slots)
        return found + [(base + n, (), 1, ways - 1, a) for n, (_, a) in enumerate(rest)]

    feed_weights = []
    feed_pieces = (slot(feed_weights, 0, rest_a), slot(feed_weights, 1, rest_b))
    encoded, memory, hidden, slope = call(
        functools.partial(feed_fwd_kernel, feed_pieces, len(feed_weights)),
        "feed_fwd",
        [(ints, SM)] + hbm(mid) + [(norms, VM)] + hbm(*feed_weights),
        [state, state_low] + [((ways, half, unit), BF, AN)] * 2,
        [wbuf, wbuf, fbuf(half, width), fbuf(half, width), buf(half, width), buf(ways, half, unit), buf(ways, half, unit)]
        + [buf(half, width), dma((2, 2 * count)), dma((1,)), dma((ways + 1, 2))],
        5 << 30,
    )
    mem_own = oneway(memory, "section", 0, 1)
    rest_c = doubled(doubled([(jnp.stack(after(z_c, memory)), 0)], bits, decoder_swap), core_bit, decoder_swap)
    mem_other = swap(mem_own, "dp", 1)
    dec_weights = []
    dec_pieces = (
        slot(dec_weights, 0, rest_a),
        slot(dec_weights, 1, rest_b),
        slot(dec_weights, 2, rest_c),
    )
    decoded, d_mid, mem_keep, mem_send, small, keep2, send2, keep3, send3 = call(
        functools.partial(decoder_kernel, dec_pieces, len(dec_weights)),
        "decoder",
        [(ints, SM)] + hbm(mid, mem_own, mem_other, codes[1, :half], codes[0], cots) + [(norms, VM)] + hbm(*dec_weights),
        [state_low, state, state_low, state_low, ((4, width), F32, VM)] + grads(ways, 2 * unit) + grads(ways, 4 * PAIR),
        [wbuf, wbuf, wbuf, fbuf(half, width), buf(length, width), buf(half, PAIR), buf(length, PAIR), buf(half, width)]
        + [buf(half, width)]
        + kept_bufs(ways)
        + [fbuf(half, PAIR), fbuf(8, half), fbuf(half, width), fbuf(half, width), buf(half, width), buf(half, width)]
        + [buf(width, half), buf(half, width), buf(width, half), buf(width, length), buf(ways, half, PAIR)]
        + [fbuf(half, width), fbuf(half, width), fbuf(length, width), buf(length, width)]
        + [buf(ways, width, 2 * unit), buf(ways, width, 4 * PAIR), dma((3, 2 * count)), dma((6,)), dma((4,))]
        + [dma((ways, count)), dma((ways, count))],
        40 << 30,
    )
    d_mem = oneway(add(mem_keep, swap(mem_send, "dp", 1)), "section", 1, 0)
    keep3, got3 = fold_dp(keep3, decoder_swap(send3, "dp", 1), decoder_swap)
    small, d_mid, keep2, send2 = call(
        functools.partial(feed_bwd_kernel, feed_pieces, len(feed_weights)),
        "feed_bwd",
        [(ints, SM)] + hbm(encoded, mid, d_mem, cots) + [(norms, VM)] + hbm(hidden, slope) + [(small, VM)]
        + hbm(d_mid, keep2, send2, *feed_weights),
        [((4, width), F32, VM), state] + grads(ways, 2 * unit),
        [wbuf, wbuf, fbuf(half, width), fbuf(half, width), buf(half, width), buf(half, width)]
        + [buf(ways, half, unit), buf(ways, half, unit), buf(width, half), buf(half, width), buf(width, half)]
        + [fbuf(half, width), fbuf(half, width), buf(ways, width, 2 * unit), dma((2, 2 * count)), dma((6,)), dma((ways, count))],
        8 << 30,
        input_output_aliases={9: 1, 10: 2, 11: 3},
    )
    got2 = swap(send2, "dp", 1)

    def self_bwd(pairs, kept, d_mid):
        return call(
            functools.partial(self_bwd_kernel, pieces1, len(weights1), pairs),
            "self_bwd",
            [(ints, SM)] + hbm(d_mid, code_own, *kept, normed_t, *weights1),
            [state, state_low] + grads(len(pairs), 4 * PAIR),
            [wbuf, fbuf(half, width), buf(length, PAIR)]
            + kept_bufs(len(pairs))
            + [fbuf(8, half), buf(width, length), buf(half, width), buf(width, half), buf(len(pairs), half, PAIR)]
            + [fbuf(half, width), fbuf(length, width), buf(half, width), buf(len(pairs), width, 4 * PAIR)]
            + [dma((count,)), dma((8,)), dma((len(pairs), count))],
            10 << 30,
        )

    d_own1, d_other1, keep1a, send1a = self_bwd(halves[0], kept_a, d_mid)
    keep2, got2 = after((keep2, got2), d_own1)
    keep2, got2 = fold_dp(keep2, got2)
    got1a = swap(send1a, "dp", 1)
    d_got1 = swap(d_other1, "dp", 1)
    r3 = fold_mp(keep3, got3, range(ways), decoder_swap)
    d_own2, d_other2, keep1b, send1b = self_bwd(halves[1], kept_b, d_mid)
    d_got2 = swap(d_other2, "dp", 1)
    d_x, small0 = call(
        last_kernel,
        "last",
        [(a, VM) for a in (d_own1, d_own2, d_got1, d_got2, x_own, d_mid, norms)],
        [((half, width), BF, VM), ((2, width), F32, VM)],
        [],
        1 << 30,
    )
    in_grads = rows_out(d_x)[None]
    section_out = rows_out(jnp.where(encoder, memory, decoded))[None]
    keep1a, got1a = fold_dp(keep1a, got1a)
    keep1b, got1b = fold_dp(keep1b, swap(send1b, "dp", 1))
    r2 = fold_mp(keep2, got2, range(ways))
    r1 = fold_mp(keep1a, got1a, range(middle)) + fold_mp(keep1b, got1b, range(middle, ways))
    grad_qkv = r1[:, : 3 * PAIR].reshape(1, blk, 3, -1)
    grad_out = r1[:, 3 * PAIR :].T[None]
    span = r2.shape[1] // 2
    grad_up = r2[None, :, :span]
    grad_down = r2[:, span:].T[None]
    r3 = r3.reshape(blk, 4, 2, -1)
    back = oneway(r3[:, :, 0].astype(BF), "section", 1, 0).astype(F32)
    r3 = jnp.where(encoder, back, r3[:, :, 1])
    grad_qc, grad_kvc, grad_oc = r3[:, 0], r3[:, 1:3], r3[:, 3].T
    small = jnp.concatenate([small0[0:1], small[:2], small0[1:2], small[2:]])
    small = small.reshape(6, count, ways, -1).transpose(1, 2, 0, 3)
    small = xor_order(small, me)
    small = xor_order(small.swapaxes(0, 1), place).swapaxes(0, 1)
    small = jnp.stack([small[a] for a in order])
    for bit in [1] + dp_bits()[::-1]:
        middle = small.shape[0] // 2
        small = small[:middle] + swap(small[middle:], "dp", bit)
    small = small[0, 0] + sum(swap(small[0, b], "mp", b) for b in range(1, ways))
    grad_gain = small[None, :3]
    grad_bias = jnp.stack([small[3], small[5]])[None]
    grad_ffn = small[4][None]
    return (
        section_out,
        in_grads,
        grad_qkv,
        grad_out,
        grad_up,
        grad_down,
        grad_gain,
        grad_bias,
        grad_ffn,
        grad_qc,
        grad_kvc,
        grad_oc,
    )


def solution(mesh):
    placed = (
        P("section", "dp", "mp", None),
        P(None, "dp", None),
        P("section", "dp", "mp", None),
        P("section", "dp", None, "mp"),
        P("section", "mp", "dp"),
        P("section", "dp", "mp"),
        P("section", "mp", "dp"),
        P("section", None, ("dp", "mp")),
        P("section", None, ("dp", "mp")),
        P("dp", ("section", "mp")),
        P("dp", None, ("section", "mp")),
        P(("section", "mp"), "dp"),
    )
    return jax.shard_map(
        on_device,
        mesh=mesh,
        in_specs=placed,
        out_specs=(
            P("section", "dp", "mp", None),
            P("section", "dp", "mp", None),
            P("section", "dp", None, "mp"),
            P("section", "mp", "dp"),
            P("section", "dp", "mp"),
            P("section", "mp", "dp"),
            P("section", None, ("dp", "mp")),
            P("section", None, ("dp", "mp")),
            P("section", ("dp", "mp")),
            P("dp", ("section", "mp")),
            P("dp", None, ("section", "mp")),
            P(("section", "mp"), "dp"),
        ),
        check_vma=False,
    )
```

```python
import functools

import jax
import jax.numpy as jnp
from jax import lax
from jax.experimental import pallas as pl
from jax.experimental.pallas import tpu as pltpu
from jax.sharding import PartitionSpec as P

HD = 64
PAIR = 2 * HD
EPS = 1e-05
BIG = 1e30
FACTOR = HD**-0.5
LOG2E = 1.4426950408889634
BF = jnp.bfloat16
F32 = jnp.float32
PAD = 16
VMEM_MIB = {"self_fwd": 56, "feed_fwd": 22, "decoder": 56, "feed_bwd": 56, "self_bwd": 56, "last": 56}


def swap(block, axis, bit):
    count = lax.axis_size(axis)
    return lax.ppermute(block, axis, [(i, i ^ bit) for i in range(count)])


def together(*values):
    return lax.optimization_barrier(values)


def oneway(block, axis, source, target):
    return lax.ppermute(block, axis, [(source, target)])


def dp_bits():
    count = lax.axis_size("dp")
    return [1 << b for b in range(1, count.bit_length() - 1)]


def relative_order():
    order = [0]
    for bit in dp_bits():
        order = order + [a ^ bit for a in order]
    return order + [a ^ 1 for a in order]


def after(x, *others):
    return lax.optimization_barrier((x, others))[0]


def decoder_swap(block, axis, bit):
    count = lax.axis_size(axis)
    pairs = [(count + i, count + (i ^ bit)) for i in range(count)]
    return lax.ppermute(block, ("section", axis), pairs)


def doubled(arrays, bits, move=swap):
    for bit in bits:
        arrays = arrays + [(move(x, "dp", bit), a ^ bit) for x, a in arrays]
    return arrays


def add(a, b):
    return (a.astype(F32) + b.astype(F32)).astype(BF)


def halves(x, axis=0):
    middle = x.shape[axis] // 2
    return lax.slice_in_dim(x, 0, middle, axis=axis), lax.slice_in_dim(x, middle, None, axis=axis)


def fold(keep, got, axis=0):
    (k1, k2), (g1, g2) = halves(keep, axis), halves(got, axis)
    return add(k1, g1), add(k2, g2)


def fold_dp(keep, got, move=swap):
    for bit in dp_bits()[::-1]:
        keep, send = fold(keep, got)
        got = move(send, "dp", bit)
    return keep, got


def fold_dp_rest(keep, got, move=swap):
    for bit in dp_bits()[-2::-1]:
        keep, send = fold(keep, got)
        got = move(send, "dp", bit)
    return keep, got


def fold_mp(keep, got, bit, move=swap):
    keep, send = fold(keep, got, 1)
    return keep, move(send, "mp", bit)


def total(keep, got):
    return keep[0, 0].astype(F32) + got[0, 0].astype(F32)


def rows_in(local):
    rows, span, width = local.shape
    parts = local.reshape(rows, 2, span // 2, width)
    first = (lax.axis_index("dp") & 1) == 0
    keep = jnp.where(first, parts[:, 0], parts[:, 1])
    got = swap(jnp.where(first, parts[:, 1], parts[:, 0]), "dp", 1)
    chip = jnp.where(first, jnp.concatenate([keep, got]), jnp.concatenate([got, keep]))
    return chip


def rows_out(own):
    ways = lax.axis_size("mp")
    return lax.all_to_all(own.reshape(ways, -1, own.shape[1]), "mp", 0, 0, tiled=True)


def rows_placed(chip):
    rows = chip.shape[0] // 2
    first = (lax.axis_index("dp") & 1) == 0
    keep = jnp.where(first, chip[:rows], chip[rows:])
    got = swap(jnp.where(first, chip[rows:], chip[:rows]), "dp", 1)
    return jnp.where(first, jnp.concatenate([keep, got], axis=1), jnp.concatenate([got, keep], axis=1))[None]


def xor_order(x, me):
    count = x.shape[0]
    bit = 1
    while bit < count:
        flipped = x.reshape((count // (2 * bit), 2, bit) + x.shape[1:])[:, ::-1].reshape(x.shape)
        x = jnp.where((me & bit) > 0, flipped, x)
        bit *= 2
    return x


def mm(a, b):
    return jnp.dot(a, b, preferred_element_type=F32)


def nt(a, b):
    return lax.dot_general(a, b, (((1,), (1,)), ((), ())), preferred_element_type=F32)


def stats(states):
    average = jnp.mean(states, axis=-1, keepdims=True)
    centred = states - average
    inv = lax.rsqrt(jnp.mean(centred * centred, axis=-1, keepdims=True) + EPS)
    return centred * inv, inv


def norm_fwd(states, gain, bias):
    hat, _ = stats(states)
    return (hat * gain + bias).astype(BF)


def norm_bwd(states, gain, grad):
    hat, inv = stats(states)
    e = grad * gain
    dx = inv * (
        e - jnp.mean(e, axis=-1, keepdims=True) - hat * jnp.mean(e * hat, axis=-1, keepdims=True)
    )
    return dx, jnp.sum(grad * hat, axis=0, keepdims=True), jnp.sum(grad, axis=0, keepdims=True)


def gelu_parts(pre):
    size = jnp.abs(pre)
    bell = jnp.exp2(pre * pre * (-0.5 * LOG2E))
    t = 1.0 / (1.0 + (0.3275911 * 0.5**0.5) * size)
    poly = 1.061405429 * t - 1.453152027
    poly = poly * t + 1.421413741
    poly = poly * t - 0.284496736
    poly = poly * t + 0.254829592
    tail = 0.5 * poly * t * bell
    return jnp.where(pre >= 0, 1.0 - tail, tail), 0.3989422804014327 * bell


def lanes(rows):
    return lax.broadcasted_iota(jnp.int32, (rows, PAIR), 1)


def head_part(h, real, other):
    lane = lanes(real.shape[0])
    mine = (lane >= HD) if h else (lane < HD)
    return jnp.where(mine, real.astype(F32), other).astype(BF)


def query_code(code):
    return code.astype(F32)


def key_code(code):
    lane = lanes(code.shape[0])
    return jnp.where((lane & (HD - 1)) < 4, (code.astype(F32) - 1.0) * BIG, 0.0)


def start(copies):
    for copy in copies:
        copy.start()
    return copies


def wait(copies):
    for copy in copies:
        copy.wait()


def moves(pairs, sems):
    return [pltpu.make_async_copy(a, b, sems.at[n]) for n, (a, b) in enumerate(pairs)]


def load_weights(me, refs, pieces, target, sems):
    blk = target.shape[1] // len({piece[4] for piece in pieces})
    copies = []
    for n, (ref, index, first, pairs, a, columns) in enumerate(pieces):
        rows = pl.ds(pl.multiple_of((me ^ a) * blk, blk), blk)
        place = target.at[pl.ds(first, pairs), rows, columns]
        copies.append(pltpu.make_async_copy(refs[ref].at[index], place, sems.at[n]))
    return start(copies)


def kernel_order(count):
    order = [0]
    bit = 2
    while bit < count:
        order = order + [a ^ bit for a in order]
        bit *= 2
    return order + [a ^ 1 for a in order]


def store_grad(me, staged, b, keep, send, sems):
    count = 2 * keep.shape[0]
    blk = staged.shape[1] // count
    copies = []
    for n, a in enumerate(kernel_order(count)):
        target = keep.at[n] if n < count // 2 else send.at[n - count // 2]
        rows = pl.ds(pl.multiple_of((me ^ a) * blk, blk), blk)
        copies.append(
            pltpu.make_async_copy(staged.at[b, rows, :], target.at[b], sems.at[b, n])
        )
    return copies


def attend_pair(q, k, v, code_q, code_k, b, logs):
    rows = q.shape[0]
    wide_v = jnp.concatenate([v, jnp.ones_like(v)], axis=1)
    scale = FACTOR * LOG2E
    outs = []
    for h in range(2):
        qa = head_part(h, q, query_code(code_q))
        ka = head_part(h, k, key_code(code_k))
        s = nt(qa, ka)
        top = jnp.max(s, axis=1, keepdims=True)
        p = jnp.exp2((s - top) * scale).astype(BF)
        o = mm(p, wide_v)
        total = o[:, PAIR:]
        outs.append(o[:, :PAIR] / total)
        logs[...] = jnp.where(lanes(rows) == 2 * b + h, top * scale + jnp.log2(total), logs[...])
    return jnp.where(lanes(rows) < HD, outs[0], outs[1])


def attend_pair_back(q, k, v, att, do, code_q, code_k, logs_ref, b):
    rows = q.shape[0]
    scale = FACTOR * LOG2E
    k_t = k.T
    prod = do.astype(F32) * att
    high = prod.astype(BF)
    low = (prod - high.astype(F32)).astype(BF)
    row = lax.broadcasted_iota(jnp.int32, (8, PAIR), 0)
    lane = lax.broadcasted_iota(jnp.int32, (8, PAIR), 1)
    pick = jnp.where((lane // HD) == row, 1.0, 0.0).astype(BF)
    delta = nt(pick, high) + nt(pick, low)
    dk = dv = 0.0
    dq_t = []
    for h in range(2):
        qa = head_part(h, q, query_code(code_q))
        ka = head_part(h, k, key_code(code_k))
        qm = head_part(h, q, 0.0)
        dm = head_part(h, do, 0.0)
        log = logs_ref[pl.ds(2 * b + h, 1), :]
        p_t = jnp.exp2(nt(ka, qa) * scale - log)
        ds_t = (p_t * (nt(v, dm) - delta[h : h + 1])).astype(BF)
        dv = dv + mm(p_t.astype(BF), dm)
        dk = dk + mm(ds_t, qm)
        dq_t.append(mm(k_t, ds_t))
    sub = lax.broadcasted_iota(jnp.int32, (PAIR, rows), 0)
    dq = jnp.where(sub < HD, dq_t[0], dq_t[1]).T
    return (dq * FACTOR).astype(BF), (dk * FACTOR).astype(BF), dv.astype(BF)


def columns(wbuf, pairs, at):
    return jnp.concatenate([wbuf[b, :, at * PAIR : (at + 1) * PAIR] for b in pairs], axis=1)


def lane_pairs(x, count):
    return [x[:, n * PAIR : (n + 1) * PAIR] for n in range(count)]


def attention_fwd(pairs, q_src, kv_src, code_q, code_k, wbuf, q_buf, k_buf, v_buf, att_buf, logs, total, emit):
    count = len(pairs)
    logs[...] = jnp.zeros_like(logs)
    queries = mm(q_src[...], columns(wbuf, pairs, 0)).astype(BF)
    for n, q in enumerate(lane_pairs(queries, count)):
        q_buf[n] = q
    for n, b in enumerate(pairs):
        kv = mm(kv_src[...], wbuf[b, :, PAIR : 3 * PAIR]).astype(BF)
        k_buf[n] = kv[:, :PAIR]
        v_buf[n] = kv[:, PAIR:]
        att_buf[n] = attend_pair(
            q_buf[n], k_buf[n], v_buf[n], code_q[...], code_k[...], n, logs
        )
        emit(n)
    attended = jnp.concatenate([att_buf[n].astype(BF) for n in range(count)], axis=1)
    total[...] += nt(attended, columns(wbuf, pairs, 3))


def attention_bwd(me, pairs, low, low_t, q_src_t, kv_src_t, code_q, code_k, wbuf, q_buf, k_buf, v_buf, att_buf, logs, do_buf, d_q_src, d_kv_src, staged, store):
    count = len(pairs)
    for n, do in enumerate(lane_pairs(mm(low[...], columns(wbuf, pairs, 3)).astype(BF), count)):
        do_buf[n] = do
    attended = jnp.concatenate([att_buf[n].astype(BF) for n in range(count)], axis=1)
    for n, part in enumerate(lane_pairs(mm(low_t[...], attended).astype(BF), count)):
        staged[n, :, 3 * PAIR :] = part
    dqs = []
    for n, b in enumerate(pairs):
        dq, dk, dv = attend_pair_back(
            q_buf[n], k_buf[n], v_buf[n], att_buf[n], do_buf[n], code_q[...], code_k[...], logs, n
        )
        dqs.append(dq)
        dkv = jnp.concatenate([dk, dv], axis=1)
        staged[n, :, PAIR : 3 * PAIR] = mm(kv_src_t[...], dkv).astype(BF)
        part = nt(dkv, wbuf[b, :, PAIR : 3 * PAIR])
        d_kv_src[...] = part if n == 0 else d_kv_src[...] + part
    dq = jnp.concatenate(dqs, axis=1)
    for n, part in enumerate(lane_pairs(mm(q_src_t[...], dq).astype(BF), count)):
        staged[n, :, :PAIR] = part
    copies = []
    for n in range(count):
        copies += start(store(n))
    d_q_src[...] = nt(dq, columns(wbuf, pairs, 0))
    return copies


def self_fwd_kernel(pieces, n_weights, ints, x_own, x_other, code_in, *refs):
    weights, refs = refs[:n_weights], refs[n_weights:]
    q_ref, k_ref, v_ref, att_ref, logs_ref, mid_ref, normed_t_ref, norms = refs[:8]
    wbuf, own, other, code, normed, mid, q_buf, k_buf, v_buf, att_buf, logs, logs_t, turned, lines, wsems, sems, osems, lsems = refs[8:]
    me = ints[0]
    half = own.shape[0]
    loads = start(moves([(x_own, own), (x_other, other), (code_in, code)], sems))
    blk = wbuf.shape[1] // n_weights
    line_copies = start(
        moves([(w.at[:, pl.ds(blk, PAD), :], lines.at[n]) for n, w in enumerate(weights)], lsems)
    )
    weight_copies = load_weights(me, weights, pieces, wbuf, wsems)
    wait(line_copies)
    parts = jnp.sum(lines[...].astype(F32), axis=(0, 1))
    norms[...] = parts[:8] + parts[8:]
    wait(loads)
    states = own[...].astype(F32)
    mid[...] = states
    normed[:half] = norm_fwd(states, norms[0:1], norms[3:4])
    normed[half:] = norm_fwd(other[...].astype(F32), norms[0:1], norms[3:4])
    wait(weight_copies)
    outs = []

    def emit(n):
        sources = [(q_buf, q_ref), (k_buf, k_ref), (v_buf, v_ref), (att_buf, att_ref)]
        outs.extend(start(moves([(a.at[n], b.at[n]) for a, b in sources], osems.at[n])))

    pairs = list(range(wbuf.shape[0]))
    attention_fwd(
        pairs, normed.at[:half], normed, code.at[:half], code, wbuf, q_buf, k_buf, v_buf, att_buf, logs, mid, emit
    )
    outs.extend(start(moves([(mid, mid_ref)], osems.at[len(pairs)])))
    logs_t[...] = logs[...].T[: logs_t.shape[0]]
    turned[...] = normed[...].T
    outs.extend(start(moves([(logs_t, logs_ref), (turned, normed_t_ref)], osems.at[len(pairs) + 1])))
    wait(outs)


def self_bwd_kernel(pieces, n_weights, pairs, ints, d_mid_in, code_in, q_in, k_in, v_in, att_in, logs_in, normed_t_in, *refs):
    weights, refs = refs[:n_weights], refs[n_weights:]
    d_own_ref, d_other_ref, keep, send = refs[:4]
    wbuf, d_mid, code, q_buf, k_buf, v_buf, att_buf, logs, normed_t, low, low_t, do_buf, d_q, d_kv, d_other, staged, wsems, sems, gsems = refs[4:]
    me = ints[0]
    half = d_mid.shape[0]
    loads = start(
        moves(
            [(d_mid_in, d_mid), (code_in, code), (q_in, q_buf), (k_in, k_buf), (v_in, v_buf), (att_in, att_buf), (logs_in, logs), (normed_t_in, normed_t)],
            sems,
        )
    )
    weight_copies = load_weights(me, weights, pieces, wbuf, wsems)
    wait(loads[:1])
    low[...] = d_mid[...].astype(BF)
    low_t[...] = low[...].T
    wait(loads[1:])
    wait(weight_copies)

    def store(n):
        return store_grad(me, staged, n, keep, send, gsems)

    copies = attention_bwd(
        me, pairs, low, low_t, normed_t.at[:, :half], normed_t, code.at[:half], code, wbuf, q_buf, k_buf, v_buf, att_buf, logs, do_buf, d_q, d_kv, staged, store
    )
    d_other[...] = d_kv[half:].astype(BF)
    outs = start(moves([(d_other, d_other_ref)], sems.at[pl.ds(0, 1)]))
    d_q[...] += d_kv[:half]
    outs += start(moves([(d_q, d_own_ref)], sems.at[pl.ds(1, 1)]))
    wait(outs + copies)


def feed_fwd_kernel(pieces, n_weights, ints, mid_in, norms, *refs):
    weights, refs = refs[:n_weights], refs[n_weights:]
    out_ref, memory_ref, hidden_ref, slope_ref = refs[:4]
    both, mid, out, memory, hidden_buf, slope_buf, normed, wsems, sems, osems = refs[4:]
    me = ints[0]

    @pl.when(ints[1] == 1)
    def _():
        loads = start(moves([(mid_in, mid)], sems))
        weight_copies = load_weights(me, weights, pieces, both, wsems)
        wait(loads)
        normed[...] = norm_fwd(mid[...], norms[1:2], norms[4:5])
        wait(weight_copies)
        outs = []
        ways, _, unit = both.shape
        unit = unit // 2
        for b in range(ways):
            pre = mm(normed[...], both[b, :, :unit])
            cdf, density = gelu_parts(pre)
            hidden_buf[b] = (pre * cdf).astype(BF)
            slope_buf[b] = (cdf + pre * density).astype(BF)
            base = mid[...] if b == 0 else out[...]
            out[...] = base + nt(hidden_buf[b], both[b, :, unit:])
            outs += start(
                moves([(hidden_buf.at[b], hidden_ref.at[b]), (slope_buf.at[b], slope_ref.at[b])], osems.at[b])
            )
        outs += start(moves([(out, out_ref)], osems.at[ways]))
        memory[...] = norm_fwd(out[...], norms[2:3], norms[5:6])
        outs += start(moves([(memory, memory_ref)], sems))
        wait(outs)


def decoder_kernel(pieces, n_weights, ints, mid_in, mem_own, mem_other, code_q_in, code_k_in, cots_in, norms, *refs):
    weights, refs = refs[:n_weights], refs[n_weights:]
    decoded_ref, d_mid_ref, mem_keep, mem_send, small, keep_u, send_u, keep_d, send_d, keep3, send3 = refs[:11]
    (
        wbuf, both, mid, mem, code_q, code_k, cots, cross_in, q_buf, k_buf, v_buf, att_buf, logs, logs_t,
        joined, out, decoded, normed, normed_t, low, low_t, mem_t, do_buf, d_norm, d_q, d_kv, d_mem,
        staged_u, staged_d, staged3, wsems, sems, osems, gsems_u, gsems_d, gsems3,
    ) = refs[11:]
    me = ints[0]
    half = mid.shape[0]

    @pl.when(ints[1] == 0)
    def _():
        loads = start(
            moves(
                [(mid_in, mid), (mem_own, mem.at[:half]), (mem_other, mem.at[half:]), (code_q_in, code_q), (code_k_in, code_k), (cots_in, cots)],
                sems,
            )
        )
        crosses = load_weights(me, weights, pieces[0], wbuf, wsems.at[0])
        feeds = load_weights(me, weights, pieces[1], both, wsems.at[1])
        pairs = list(range(wbuf.shape[0]))
        wait(loads[:1])
        joined[...] = mid[...]
        cross_in[...] = norm_fwd(mid[...], norms[2:3], norms[5:6])
        wait(loads[1:])
        wait(crosses)
        attention_fwd(
            pairs, cross_in, mem, code_q, code_k, wbuf, q_buf, k_buf, v_buf, att_buf, logs, joined, lambda n: None
        )
        logs_t[...] = logs[...].T[: logs_t.shape[0]]
        wait(feeds)
        normed[...] = norm_fwd(joined[...], norms[1:2], norms[4:5])
        normed_t[...] = normed[...].T
        low_t[...] = cots[...].T
        unit = both.shape[2] // 2
        copies = []
        for b in pairs:
            pre = mm(normed[...], both[b, :, :unit])
            cdf, density = gelu_parts(pre)
            hidden = (pre * cdf).astype(BF)
            base = joined[...] if b == 0 else out[...]
            out[...] = base + nt(hidden, both[b, :, unit:])
            d_pre = (mm(cots[...], both[b, :, unit:]) * (cdf + pre * density)).astype(BF)
            staged_u[b] = mm(normed_t[...], d_pre).astype(BF)
            copies += start(store_grad(me, staged_u, b, keep_u, send_u, gsems_u))
            staged_d[b] = mm(low_t[...], hidden).astype(BF)
            copies += start(store_grad(me, staged_d, b, keep_d, send_d, gsems_d))
            part = nt(d_pre, both[b, :, :unit])
            d_norm[...] = part if b == 0 else d_norm[...] + part
        decoded[...] = out[...].astype(BF)
        outs = start(moves([(decoded, decoded_ref)], osems))
        dx, d_gain1, d_bias1 = norm_bwd(joined[...], norms[1:2], d_norm[...])
        joined[...] = cots[...].astype(F32) + dx
        def store3(n):
            return store_grad(me, staged3, n, keep3, send3, gsems3)

        low[...] = joined[...].astype(BF)
        low_t[...] = low[...].T
        mem_t[...] = mem[...].T
        normed_t[...] = cross_in[...].T
        copies += attention_bwd(
            me, pairs, low, low_t, normed_t, mem_t, code_q, code_k, wbuf, q_buf, k_buf, v_buf, att_buf, logs_t, do_buf, d_q, d_kv, staged3, store3
        )
        d_mem[...] = d_kv[...].astype(BF)
        outs += start(
            moves([(d_mem.at[half:], mem_send), (d_mem.at[:half], mem_keep)], osems.at[pl.ds(1, 2)])
        )
        dx, d_gain2, d_bias2 = norm_bwd(mid[...], norms[2:3], d_q[...])
        out[...] = joined[...] + dx
        outs += start(moves([(out, d_mid_ref)], osems.at[pl.ds(3, 1)]))
        small[0:1] = d_gain1
        small[1:2] = d_gain2
        small[2:3] = d_bias1
        small[3:4] = d_bias2
        wait(outs + copies)


def feed_bwd_kernel(pieces, n_weights, ints, encoded_in, mid_in, d_mem_in, cots_in, norms, hidden_in, slope_in, small_in, d_mid_in, keep_u_in, send_u_in, keep_d_in, send_d_in, *refs):
    weights, refs = refs[:n_weights], refs[n_weights:]
    small, d_mid_ref, keep_u, send_u, keep_d, send_d = refs[:6]
    (
        both, encoded, mid, d_mem, cots, hidden, slope, normed_t, low, low_t, d_out, d_norm, staged_u, staged_d, wsems, sems, gsems_u, gsems_d,
    ) = refs[6:]
    me = ints[0]

    @pl.when(ints[1] == 0)
    def _():
        small[...] = small_in[...]

    @pl.when(ints[1] == 1)
    def _():
        loads = start(
            moves(
                [(encoded_in, encoded), (d_mem_in, d_mem), (cots_in, cots), (mid_in, mid), (hidden_in, hidden), (slope_in, slope)],
                sems,
            )
        )
        weight_copies = load_weights(me, weights, pieces, both, wsems)
        wait(loads[:3])
        grad = d_mem[...].astype(F32) + cots[...].astype(F32)
        dx, d_gain, d_bias = norm_bwd(encoded[...], norms[2:3], grad)
        small[1:2] = d_gain
        small[3:4] = d_bias
        d_out[...] = dx
        low[...] = dx.astype(BF)
        low_t[...] = low[...].T
        wait(loads[3:])
        normed_t[...] = norm_fwd(mid[...], norms[1:2], norms[4:5]).T
        wait(weight_copies)
        ways, _, unit = both.shape
        unit = unit // 2
        copies = []
        for b in range(ways):
            d_pre = (mm(low[...], both[b, :, unit:]) * slope[b].astype(F32)).astype(BF)
            staged_u[b] = mm(normed_t[...], d_pre).astype(BF)
            copies += start(store_grad(me, staged_u, b, keep_u, send_u, gsems_u))
            staged_d[b] = mm(low_t[...], hidden[b]).astype(BF)
            copies += start(store_grad(me, staged_d, b, keep_d, send_d, gsems_d))
            part = nt(d_pre, both[b, :, :unit])
            d_norm[...] = part if b == 0 else d_norm[...] + part
        dx, d_gain1, d_bias1 = norm_bwd(mid[...], norms[1:2], d_norm[...])
        d_out[...] += dx
        outs = start(moves([(d_out, d_mid_ref)], sems))
        small[0:1] = d_gain1
        small[2:3] = d_bias1
        wait(outs + copies)


def last_kernel(d_own, d_got, x_own, d_mid, norms, dx_ref, small):
    grad = d_own[...] + d_got[...].astype(F32)
    dx, d_gain, d_bias = norm_bwd(x_own[...].astype(F32), norms[0:1], grad)
    dx_ref[...] = (d_mid[...] + dx).astype(BF)
    small[0:1] = d_gain
    small[1:2] = d_bias


VM = pl.BlockSpec(memory_space=pltpu.VMEM)
SM = pl.BlockSpec(memory_space=pltpu.SMEM)
AN = pl.BlockSpec(memory_space=pl.ANY)


def call(kernel, name, ins, outs, scratch, flops, **more):
    return pl.pallas_call(
        kernel,
        name=name,
        in_specs=[spec for _, spec in ins],
        out_shape=[jax.ShapeDtypeStruct(shape, dtype) for shape, dtype, _ in outs],
        out_specs=[spec for _, _, spec in outs],
        scratch_shapes=scratch,
        compiler_params=pltpu.CompilerParams(vmem_limit_bytes=VMEM_MIB[name] << 20),
        cost_estimate=pl.CostEstimate(flops=flops, bytes_accessed=8 << 20, transcendentals=0),
        **more,
    )(*[array for array, _ in ins])


def on_device(layer_in, segment_ids, out_grads, w_qkv, w_out, w_up, w_down, norm_gain, norm_bias, w_qc, w_kvc, w_oc):
    encoder = lax.axis_index("section") == 0
    me = lax.axis_index("dp")
    core = me & 1
    place = lax.axis_index("mp")
    ways = lax.axis_size("mp")
    count = lax.axis_size("dp")
    rows = layer_in.shape[1]
    width = layer_in.shape[3]
    blk = w_qkv.shape[1]
    half = 2 * layer_in.shape[2]
    length = 2 * half
    assert rows == 2 and ways == 4 and length == segment_ids.shape[2]
    ints = jnp.stack([me, encoder.astype(jnp.int32), place])

    each = norm_gain.shape[2]
    spread = jnp.tile(jnp.concatenate([norm_gain[0], norm_bias[0]]), (1, width // each))
    spread = jnp.where(jnp.arange(width) // each == me * ways + place, spread, 0.0)
    high = spread.astype(BF)
    low = (spread - high.astype(F32)).astype(BF)
    gap = jnp.zeros((2, width), BF)
    shard1 = jnp.concatenate([w_qkv[0].reshape(blk, -1), w_out[0].T], axis=1)
    shard1 = jnp.concatenate([shard1, high, gap, low, gap])
    bits, core_bit = dp_bits(), [1]
    unit = w_up.shape[2]
    shard2 = jnp.concatenate([w_up[0], w_down[0].T], axis=1)
    mine3 = jnp.stack([w_qc, w_kvc[:, 0], w_kvc[:, 1], w_oc.T], axis=1)
    theirs3 = oneway(mine3, "section", 0, 1)
    pair1 = jnp.stack([shard1, swap(shard1, "mp", 2)])
    own2, held2 = shard2[None], [0]
    for bit in bits:
        own2 = jnp.concatenate([own2, swap(own2, "dp", bit)])
        held2 = held2 + [a ^ bit for a in held2]
    up_pair = jnp.stack([w_up[0], swap(w_up[0], "mp", 2)])
    x_own = lax.all_to_all(rows_in(layer_in[0]), "mp", 0, 0, tiled=True).reshape(-1, width)
    cots = lax.all_to_all(after(rows_in(out_grads[0]), x_own), "mp", 0, 0, tiled=True).reshape(-1, width)
    pair1 = after(pair1, x_own)
    all1 = jnp.concatenate([pair1, swap(pair1, "mp", 1)])
    own3 = after(jnp.concatenate([theirs3, mine3], axis=2).reshape(1, blk, -1), pair1)
    for bit in bits:
        own3 = jnp.concatenate([own3, decoder_swap(own3, "dp", bit)])
    w1 = doubled([(all1, 0)], bits)
    up_pair, own2 = after((up_pair, own2), all1)
    up_rest = jnp.concatenate([up_pair[1:], swap(up_pair, "mp", 1)])
    down_own = own2[:, :, unit:]
    down_pair = jnp.stack([down_own, swap(down_own, "mp", 2)])
    up_rest, down_pair = after((up_rest, down_pair), *[w for w, _ in w1])
    w1 = doubled(w1, core_bit)
    x_other = swap(x_own, "dp", 1)

    other_segs = swap(segment_ids, "dp", 1)
    segs = jnp.where(core == (place >> 1), segment_ids, other_segs)
    segs = jnp.where((place & 1) == 0, segs[:, 0], segs[:, 1])
    segs = segs.reshape(2, ways, 2, -1).transpose(0, 2, 1, 3)
    segs = jnp.where(core == 0, segs, segs[:, ::-1]).reshape(2, length)
    lane = jnp.arange(PAIR) & (HD - 1)
    codes = (segs[:, :, None] == lane[None, None, :]).astype(BF)
    code_own = jnp.where(encoder, codes[0], codes[1])

    middle = ways // 2
    dma = pltpu.SemaphoreType.DMA

    def buf(*shape):
        return pltpu.VMEM(shape, BF)

    def fbuf(*shape):
        return pltpu.VMEM(shape, F32)

    def hbm(*arrays):
        return [(a, AN) for a in arrays]

    wbuf = buf(ways, width, 4 * PAIR)
    rows1, every = (pl.ds(0, ways), pl.ds(0, blk)), pl.ds(0, 4 * PAIR)
    pieces1 = [(n, rows1, 0, ways, a, every) for n, (_, a) in enumerate(w1)]

    weights1 = [w for w, _ in w1]

    def kept_shapes(count):
        return [
            ((count, half, PAIR), BF, AN),
            ((count, length, PAIR), BF, AN),
            ((count, length, PAIR), BF, AN),
            ((count, half, PAIR), F32, AN),
            ((8, half), F32, AN),
        ]

    def kept_bufs(count):
        return [buf(count, half, PAIR), buf(count, length, PAIR), buf(count, length, PAIR), fbuf(count, half, PAIR)]

    def grads(pairs, columns):
        return [((count // 2, pairs, blk, columns), BF, AN)] * 2

    state, state_low = ((half, width), F32, AN), ((half, width), BF, AN)

    x_other, cots = together(x_other, cots)
    up_rests = doubled([(up_rest, 0)], bits)
    down_rest = jnp.concatenate([down_pair[1:], swap(down_pair, "mp", 1)])
    pair3 = jnp.stack([own3, decoder_swap(own3, "mp", 2)])
    *kept, mid, normed_t, norms = call(
        functools.partial(self_fwd_kernel, pieces1, len(weights1)),
        "self_fwd",
        [(ints, SM)] + hbm(x_own, x_other, code_own, *weights1),
        kept_shapes(ways) + [state, ((width, length), BF, AN), ((8, width), F32, VM)],
        [wbuf, buf(half, width), buf(half, width), buf(length, PAIR), buf(length, width), fbuf(half, width)]
        + kept_bufs(ways)
        + [fbuf(half, PAIR), fbuf(8, half), buf(width, length), buf(count, ways, PAD, width)]
        + [dma((count,)), dma((3,)), dma((ways + 2, 4)), dma((count,))],
        5 << 30,
    )
    mid, pair3, own2, down_rest, *arrays = together(mid, pair3, own2, down_rest, *[w for w, _ in up_rests])
    up_rests = [(w, a) for w, (_, a) in zip(arrays, up_rests)]
    weights2 = [w for w, _ in doubled([(own2, 0), (down_rest, 0)] + up_rests, core_bit)]
    pieces2 = []
    others, low, high = pl.ds(0, ways - 1), pl.ds(0, unit), pl.ds(unit, unit)
    for n in range(2):
        base = n * (2 + len(up_rests))
        for at, a in enumerate(held2):
            pieces2.append((base, (pl.ds(at, 1),), 0, 1, a ^ n, pl.ds(0, 2 * unit)))
            pieces2.append((base + 1, (others, at), 1, ways - 1, a ^ n, high))
        for at, (_, a) in enumerate(up_rests):
            pieces2.append((base + 2 + at, (others,), 1, ways - 1, a ^ n, low))
    all3 = jnp.concatenate([pair3, decoder_swap(pair3, "mp", 1)])
    wbuf2 = buf(ways, width, 2 * unit)
    encoded, memory, hidden, slope = call(
        functools.partial(feed_fwd_kernel, pieces2, len(weights2)),
        "feed_fwd",
        [(ints, SM)] + hbm(mid) + [(norms, VM)] + hbm(*weights2),
        [state, state_low] + [((ways, half, unit), BF, AN)] * 2,
        [wbuf2, fbuf(half, width), fbuf(half, width), buf(half, width), buf(ways, half, unit), buf(ways, half, unit)]
        + [buf(half, width), dma((3 * count,)), dma((1,)), dma((ways + 1, 2))],
        5 << 30,
    )
    mem_own = oneway(memory, "section", 0, 1)
    mem_other = swap(mem_own, "dp", 1)
    w3 = doubled([(after(all3, mem_own), 0)], core_bit, decoder_swap)
    weights3 = [w for w, _ in w3]
    pieces3 = [(n, (pl.ds(0, ways), at), 0, ways, a ^ n, every) for n in range(2) for at, a in enumerate(held2)]
    dec_pieces = (pieces3, [(len(weights3) + piece[0],) + piece[1:] for piece in pieces2])
    decoded, d_mid, mem_keep, mem_send, small, keep_u, send_u, keep_d, send_d, keep3, send3 = call(
        functools.partial(decoder_kernel, dec_pieces, len(weights3) + len(weights2)),
        "decoder",
        [(ints, SM)] + hbm(mid, mem_own, mem_other, codes[1, :half], codes[0], cots) + [(norms, VM)] + hbm(*weights3, *weights2),
        [state_low, state, state_low, state_low, ((4, width), F32, VM)] + grads(ways, unit) * 2
        + grads(ways, 4 * PAIR),
        [wbuf, wbuf2, fbuf(half, width), buf(length, width), buf(half, PAIR), buf(length, PAIR), buf(half, width)]
        + [buf(half, width)]
        + kept_bufs(ways)
        + [fbuf(half, PAIR), fbuf(8, half), fbuf(half, width), fbuf(half, width), buf(half, width), buf(half, width)]
        + [buf(width, half), buf(half, width), buf(width, half), buf(width, length), buf(ways, half, PAIR)]
        + [fbuf(half, width), fbuf(half, width), fbuf(length, width), buf(length, width)]
        + [buf(ways, width, unit), buf(ways, width, unit), buf(ways, width, 4 * PAIR), dma((2, 3 * count)), dma((6,))]
        + [dma((4,)), dma((ways, count)), dma((ways, count)), dma((ways, count))],
        40 << 30,
    )
    mem_sum = add(mem_keep, swap(mem_send, "dp", 1))
    d_mem = oneway(mem_sum, "section", 1, 0)
    got3 = decoder_swap(after(send3, mem_sum), "dp", 1)
    section_out = rows_out(jnp.where(encoder, memory, after(decoded, mem_sum)))
    d_mem, got3, section_out = together(d_mem, got3, section_out)
    bit = bits[-1]
    keep3, send3 = fold(keep3, got3)
    small, d_mid, keep_u, send_u, keep_d, send_d = call(
        functools.partial(feed_bwd_kernel, pieces2, len(weights2)),
        "feed_bwd",
        [(ints, SM)] + hbm(encoded, mid, d_mem, cots) + [(norms, VM)] + hbm(hidden, slope) + [(small, VM)]
        + hbm(d_mid, keep_u, send_u, keep_d, send_d, *weights2),
        [((4, width), F32, VM), state] + grads(ways, unit) * 2,
        [wbuf2, fbuf(half, width), fbuf(half, width), buf(half, width), buf(half, width)]
        + [buf(ways, half, unit), buf(ways, half, unit), buf(width, half), buf(half, width), buf(width, half)]
        + [fbuf(half, width), fbuf(half, width), buf(ways, width, unit), buf(ways, width, unit), dma((3 * count,)), dma((6,))]
        + [dma((ways, count)), dma((ways, count))],
        8 << 30,
        input_output_aliases={9: 1, 10: 2, 11: 3, 12: 4, 13: 5},
    )
    got_u, got_d = swap(send_u, "dp", 1), swap(send_d, "dp", 1)
    got3 = decoder_swap(after(send3, d_mem), "dp", bit)

    def self_bwd(pairs, kept, d_mid):
        return call(
            functools.partial(self_bwd_kernel, pieces1, len(weights1), pairs),
            "self_bwd",
            [(ints, SM)] + hbm(d_mid, code_own, *kept, normed_t, *weights1),
            [state, state_low] + grads(len(pairs), 4 * PAIR),
            [wbuf, fbuf(half, width), buf(length, PAIR)]
            + kept_bufs(len(pairs))
            + [fbuf(8, half), buf(width, length), buf(half, width), buf(width, half), buf(len(pairs), half, PAIR)]
            + [fbuf(half, width), fbuf(length, width), buf(half, width), buf(len(pairs), width, 4 * PAIR)]
            + [dma((count,)), dma((8,)), dma((len(pairs), count))],
            10 << 30,
        )

    got_u, got_d, got3 = together(got_u, got_d, got3)
    keep_u, send_u = fold(keep_u, got_u)
    keep_d, send_d = fold(keep_d, got_d, 1)
    got_u, got_d = swap(send_u, "dp", bit), swap(send_d, "mp", 1)
    keep3, got3 = fold_dp_rest(keep3, got3, decoder_swap)
    keep3, send3 = fold(keep3, got3, 1)
    got3 = decoder_swap(send3, "mp", 1)
    d_own, d_other, keep1, send1 = self_bwd(list(range(ways)), kept, after(d_mid, send_u, send_d, send3))
    d_other, send1, got_u, got_d, got3 = together(d_other, send1, got_u, got_d, got3)
    got1 = swap(send1, "dp", 1)
    d_got = swap(d_other, "dp", 1)
    keep3, got3 = fold_mp(keep3, got3, 2, decoder_swap)
    keep1, send1 = fold(keep1, got1)
    keep_u, got_u, keep_d, got_d = after((keep_u, got_u, keep_d, got_d), send1)
    keep_d, send_d = fold(keep_d, got_d)
    got = swap(jnp.concatenate([send1, send_d], axis=1), "dp", bit)
    keep_u, got_u = fold_dp_rest(keep_u, got_u)
    keep_u, send_u = fold(keep_u, got_u, 1)
    got_u = swap(send_u, "mp", 1)
    d_own = after(d_own, send1, send_u, send_d)
    d_x, small0 = call(
        last_kernel,
        "last",
        [(a, VM) for a in (d_own, d_got, x_own, d_mid, norms)],
        [((half, width), BF, VM), ((2, width), F32, VM)],
        [],
        1 << 30,
    )
    in_grads = rows_out(d_x)
    d_x, small0, got, got_u, got3 = together(d_x, small0, got, got_u, got3)
    small = jnp.concatenate([small0[0:1], small[:2], small0[1:2], small[2:]])
    order = relative_order()
    small = small.reshape(6, count, ways, -1).transpose(1, 2, 0, 3)
    small = xor_order(small, me)
    small = xor_order(small.swapaxes(0, 1), place)
    small = jnp.stack([small[n] for n in (0, 2, 1, 3)], axis=1)
    small = jnp.stack([small[a] for a in order])
    for turn in [1] + bits[::-1]:
        small, send = halves(small)
        small = small + swap(send, "dp", turn)
    small = small.reshape(1, ways, 1, -1)
    small = jnp.pad(small, ((0, 0), (0, 0), (0, PAD - 1), (0, 4 * PAIR - small.shape[3])))
    keep1, got1 = fold_dp_rest(keep1, got[:, :ways])
    keep_d, got_d = fold_dp_rest(keep_d, got[:, ways:])
    keep1, send1 = fold(keep1, got1, 1)
    small_keep, small_send = halves(small.astype(BF), 1)
    send1 = jnp.concatenate([send1, small_send], axis=2)
    got1 = swap(send1, "mp", 1)
    keep1 = jnp.concatenate([keep1, small_keep], axis=2)
    r3 = total(keep3, got3).reshape(blk, 4, 2, -1)
    back = oneway(after(r3[:, :, 0].astype(BF), send1), "section", 1, 0)
    keep_u, send_u = fold(keep_u, got_u, 1)
    keep_d, send_d = fold(keep_d, got_d, 1)
    got = swap(jnp.concatenate([send_u, send_d], axis=1), "mp", 2)
    keep1, send1 = fold(keep1, got1, 1)
    got1 = swap(send1, "mp", 2)
    got, back, in_grads = after((got, back, in_grads), send1)
    got_u, got_d = halves(got, 1)
    r_up, r_down, r1 = total(keep_u, got_u), total(keep_d, got_d), total(keep1, got1)
    small, r1 = r1[blk, : 6 * each].reshape(6, each), r1[:blk]
    section_out, in_grads = rows_placed(section_out), rows_placed(in_grads)
    grad_qkv = r1[:, : 3 * PAIR].reshape(1, blk, 3, -1)
    grad_out = r1[:, 3 * PAIR :].T[None]
    grad_up = r_up[None]
    grad_down = r_down.T[None]
    r3 = jnp.where(encoder, back.astype(F32), r3[:, :, 1])
    grad_qc, grad_kvc, grad_oc = r3[:, 0], r3[:, 1:3], r3[:, 3].T
    grad_gain = small[None, :3]
    grad_bias = jnp.stack([small[3], small[5]])[None]
    grad_ffn = small[4][None]
    return (
        section_out,
        in_grads,
        grad_qkv,
        grad_out,
        grad_up,
        grad_down,
        grad_gain,
        grad_bias,
        grad_ffn,
        grad_qc,
        grad_kvc,
        grad_oc,
    )


def solution(mesh):
    placed = (
        P("section", "dp", "mp", None),
        P(None, "dp", None),
        P("section", "dp", "mp", None),
        P("section", "dp", None, "mp"),
        P("section", "mp", "dp"),
        P("section", "dp", "mp"),
        P("section", "mp", "dp"),
        P("section", None, ("dp", "mp")),
        P("section", None, ("dp", "mp")),
        P("dp", ("section", "mp")),
        P("dp", None, ("section", "mp")),
        P(("section", "mp"), "dp"),
    )
    return jax.shard_map(
        on_device,
        mesh=mesh,
        in_specs=placed,
        out_specs=(
            P("section", "dp", "mp", None),
            P("section", "dp", "mp", None),
            P("section", "dp", None, "mp"),
            P("section", "mp", "dp"),
            P("section", "dp", "mp"),
            P("section", "mp", "dp"),
            P("section", None, ("dp", "mp")),
            P("section", None, ("dp", "mp")),
            P("section", ("dp", "mp")),
            P("dp", ("section", "mp")),
            P("dp", None, ("section", "mp")),
            P(("section", "mp"), "dp"),
        ),
        check_vma=False,
    )
```

```python
import functools

import jax
import jax.numpy as jnp
from jax import lax
from jax.experimental import pallas as pl
from jax.experimental.pallas import tpu as pltpu
from jax.sharding import PartitionSpec as P

HD = 64
PAIR = 2 * HD
EPS = 1e-05
BIG = 1e30
FACTOR = HD**-0.5
LOG2E = 1.4426950408889634
BF = jnp.bfloat16
F32 = jnp.float32
PAD = 16
VMEM_MIB = {"self_fwd": 56, "feed_fwd": 22, "decoder": 46, "feed_bwd": 56, "self_bwd": 56, "last": 56}


def swap(block, axis, bit):
    count = lax.axis_size(axis)
    return lax.ppermute(block, axis, [(i, i ^ bit) for i in range(count)])


def together(*values):
    return lax.optimization_barrier(values)


def oneway(block, axis, source, target):
    return lax.ppermute(block, axis, [(source, target)])


def dp_bits():
    count = lax.axis_size("dp")
    return [1 << b for b in range(1, count.bit_length() - 1)]


def relative_order():
    order = [0]
    for bit in dp_bits():
        order = order + [a ^ bit for a in order]
    return order + [a ^ 1 for a in order]


def after(x, *others):
    return lax.optimization_barrier((x, others))[0]


def decoder_swap(block, axis, bit):
    count = lax.axis_size(axis)
    pairs = [(count + i, count + (i ^ bit)) for i in range(count)]
    return lax.ppermute(block, ("section", axis), pairs)


def doubled(arrays, bits, move=swap):
    for bit in bits:
        arrays = arrays + [(move(x, "dp", bit), a ^ bit) for x, a in arrays]
    return arrays


def add(a, b):
    return (a.astype(F32) + b.astype(F32)).astype(BF)


def halves(x, axis=0):
    middle = x.shape[axis] // 2
    return lax.slice_in_dim(x, 0, middle, axis=axis), lax.slice_in_dim(x, middle, None, axis=axis)


def fold(keep, got, axis=0):
    (k1, k2), (g1, g2) = halves(keep, axis), halves(got, axis)
    return add(k1, g1), add(k2, g2)


def fold_dp(keep, got, move=swap):
    for bit in dp_bits()[::-1]:
        keep, send = fold(keep, got)
        got = move(send, "dp", bit)
    return keep, got


def fold_dp_rest(keep, got, move=swap):
    for bit in dp_bits()[-2::-1]:
        keep, send = fold(keep, got)
        got = move(send, "dp", bit)
    return keep, got


def fold_mp(keep, got, bit, move=swap):
    keep, send = fold(keep, got, 1)
    return keep, move(send, "mp", bit)


def total(keep, got):
    return keep[0, 0].astype(F32) + got[0, 0].astype(F32)


def rows_in(local):
    rows, span, width = local.shape
    parts = local.reshape(rows, 2, span // 2, width)
    first = (lax.axis_index("dp") & 1) == 0
    keep = jnp.where(first, parts[:, 0], parts[:, 1])
    got = swap(jnp.where(first, parts[:, 1], parts[:, 0]), "dp", 1)
    chip = jnp.where(first, jnp.concatenate([keep, got]), jnp.concatenate([got, keep]))
    return chip


def rows_out(own):
    ways = lax.axis_size("mp")
    return lax.all_to_all(own.reshape(ways, -1, own.shape[1]), "mp", 0, 0, tiled=True)


def rows_placed(chip):
    rows = chip.shape[0] // 2
    first = (lax.axis_index("dp") & 1) == 0
    keep = jnp.where(first, chip[:rows], chip[rows:])
    got = swap(jnp.where(first, chip[rows:], chip[:rows]), "dp", 1)
    return jnp.where(first, jnp.concatenate([keep, got], axis=1), jnp.concatenate([got, keep], axis=1))[None]


def xor_order(x, me):
    count = x.shape[0]
    bit = 1
    while bit < count:
        flipped = x.reshape((count // (2 * bit), 2, bit) + x.shape[1:])[:, ::-1].reshape(x.shape)
        x = jnp.where((me & bit) > 0, flipped, x)
        bit *= 2
    return x


def mm(a, b):
    return jnp.dot(a, b, preferred_element_type=F32)


def nt(a, b):
    return lax.dot_general(a, b, (((1,), (1,)), ((), ())), preferred_element_type=F32)


def stats(states):
    average = jnp.mean(states, axis=-1, keepdims=True)
    centred = states - average
    inv = lax.rsqrt(jnp.mean(centred * centred, axis=-1, keepdims=True) + EPS)
    return centred * inv, inv


def norm_fwd(states, gain, bias):
    hat, _ = stats(states)
    return (hat * gain + bias).astype(BF)


def norm_bwd(states, gain, grad):
    hat, inv = stats(states)
    e = grad * gain
    dx = inv * (
        e - jnp.mean(e, axis=-1, keepdims=True) - hat * jnp.mean(e * hat, axis=-1, keepdims=True)
    )
    return dx, jnp.sum(grad * hat, axis=0, keepdims=True), jnp.sum(grad, axis=0, keepdims=True)


def gelu_parts(pre):
    size = jnp.abs(pre)
    bell = jnp.exp2(pre * pre * (-0.5 * LOG2E))
    t = 1.0 / (1.0 + (0.3275911 * 0.5**0.5) * size)
    poly = 1.061405429 * t - 1.453152027
    poly = poly * t + 1.421413741
    poly = poly * t - 0.284496736
    poly = poly * t + 0.254829592
    tail = 0.5 * poly * t * bell
    return jnp.where(pre >= 0, 1.0 - tail, tail), 0.3989422804014327 * bell


def lanes(rows):
    return lax.broadcasted_iota(jnp.int32, (rows, PAIR), 1)


def head_part(h, real, other):
    lane = lanes(real.shape[0])
    mine = (lane >= HD) if h else (lane < HD)
    return jnp.where(mine, real.astype(F32), other).astype(BF)


def query_code(code):
    return code.astype(F32)


def key_code(code):
    lane = lanes(code.shape[0])
    return jnp.where((lane & (HD - 1)) < 4, (code.astype(F32) - 1.0) * BIG, 0.0)


def start(copies):
    for copy in copies:
        copy.start()
    return copies


def wait(copies):
    for copy in copies:
        copy.wait()


def moves(pairs, sems):
    return [pltpu.make_async_copy(a, b, sems.at[n]) for n, (a, b) in enumerate(pairs)]


def load_weights(me, refs, pieces, target, sems):
    blk = target.shape[1] // len({piece[4] for piece in pieces})
    copies = []
    for n, (ref, index, first, pairs, a, columns) in enumerate(pieces):
        rows = pl.ds(pl.multiple_of((me ^ a) * blk, blk), blk)
        place = target.at[pl.ds(first, pairs), rows, columns]
        copies.append(pltpu.make_async_copy(refs[ref].at[index], place, sems.at[n]))
    return start(copies)


def kernel_order(count):
    order = [0]
    bit = 2
    while bit < count:
        order = order + [a ^ bit for a in order]
        bit *= 2
    return order + [a ^ 1 for a in order]


def store_grad(me, staged, b, keep, send, sems):
    count = 2 * keep.shape[0]
    blk = staged.shape[1] // count
    copies = []
    for n, a in enumerate(kernel_order(count)):
        target = keep.at[n] if n < count // 2 else send.at[n - count // 2]
        rows = pl.ds(pl.multiple_of((me ^ a) * blk, blk), blk)
        copies.append(
            pltpu.make_async_copy(staged.at[b, rows, :], target.at[b], sems.at[b, n])
        )
    return copies


def attend_pair(q, k, v, code_q, code_k, b, logs):
    rows = q.shape[0]
    wide_v = jnp.concatenate([v, jnp.ones_like(v)], axis=1)
    scale = FACTOR * LOG2E
    outs = []
    for h in range(2):
        qa = head_part(h, q, query_code(code_q))
        ka = head_part(h, k, key_code(code_k))
        s = nt(qa, ka)
        top = jnp.max(s, axis=1, keepdims=True)
        p = jnp.exp2((s - top) * scale).astype(BF)
        o = mm(p, wide_v)
        total = o[:, PAIR:]
        outs.append(o[:, :PAIR] / total)
        logs[...] = jnp.where(lanes(rows) == 2 * b + h, top * scale + jnp.log2(total), logs[...])
    return jnp.where(lanes(rows) < HD, outs[0], outs[1])


def attend_pair_back(q, k, v, att, do, code_q, code_k, logs_ref, b):
    rows = q.shape[0]
    scale = FACTOR * LOG2E
    k_t = k.T
    prod = do.astype(F32) * att
    high = prod.astype(BF)
    low = (prod - high.astype(F32)).astype(BF)
    row = lax.broadcasted_iota(jnp.int32, (8, PAIR), 0)
    lane = lax.broadcasted_iota(jnp.int32, (8, PAIR), 1)
    pick = jnp.where((lane // HD) == row, 1.0, 0.0).astype(BF)
    delta = nt(pick, high) + nt(pick, low)
    dk = dv = 0.0
    dq_t = []
    for h in range(2):
        qa = head_part(h, q, query_code(code_q))
        ka = head_part(h, k, key_code(code_k))
        qm = head_part(h, q, 0.0)
        dm = head_part(h, do, 0.0)
        log = logs_ref[pl.ds(2 * b + h, 1), :]
        p_t = jnp.exp2(nt(ka, qa) * scale - log)
        ds_t = (p_t * (nt(v, dm) - delta[h : h + 1])).astype(BF)
        dv = dv + mm(p_t.astype(BF), dm)
        dk = dk + mm(ds_t, qm)
        dq_t.append(mm(k_t, ds_t))
    sub = lax.broadcasted_iota(jnp.int32, (PAIR, rows), 0)
    dq = jnp.where(sub < HD, dq_t[0], dq_t[1]).T
    return (dq * FACTOR).astype(BF), (dk * FACTOR).astype(BF), dv.astype(BF)


def columns(wbuf, pairs, at):
    return jnp.concatenate([wbuf[b, :, at * PAIR : (at + 1) * PAIR] for b in pairs], axis=1)


def lane_pairs(x, count):
    return [x[:, n * PAIR : (n + 1) * PAIR] for n in range(count)]


def attention_fwd(pairs, q_src, kv_src, code_q, code_k, wbuf, q_buf, k_buf, v_buf, att_buf, logs, total, emit):
    count = len(pairs)
    logs[...] = jnp.zeros_like(logs)
    queries = mm(q_src[...], columns(wbuf, pairs, 0)).astype(BF)
    for n, q in enumerate(lane_pairs(queries, count)):
        q_buf[n] = q
    for n, b in enumerate(pairs):
        kv = mm(kv_src[...], wbuf[b, :, PAIR : 3 * PAIR]).astype(BF)
        k_buf[n] = kv[:, :PAIR]
        v_buf[n] = kv[:, PAIR:]
        att_buf[n] = attend_pair(
            q_buf[n], k_buf[n], v_buf[n], code_q[...], code_k[...], n, logs
        )
        emit(n)
    attended = jnp.concatenate([att_buf[n].astype(BF) for n in range(count)], axis=1)
    total[...] += nt(attended, columns(wbuf, pairs, 3))


def attention_bwd(me, pairs, low, low_t, q_src_t, kv_src_t, code_q, code_k, wbuf, q_buf, k_buf, v_buf, att_buf, logs, do_buf, d_q_src, d_kv_src, staged, store):
    count = len(pairs)
    for n, do in enumerate(lane_pairs(mm(low[...], columns(wbuf, pairs, 3)).astype(BF), count)):
        do_buf[n] = do
    attended = jnp.concatenate([att_buf[n].astype(BF) for n in range(count)], axis=1)
    for n, part in enumerate(lane_pairs(mm(low_t[...], attended).astype(BF), count)):
        staged[n, :, 3 * PAIR :] = part
    dqs = []
    for n, b in enumerate(pairs):
        dq, dk, dv = attend_pair_back(
            q_buf[n], k_buf[n], v_buf[n], att_buf[n], do_buf[n], code_q[...], code_k[...], logs, n
        )
        dqs.append(dq)
        dkv = jnp.concatenate([dk, dv], axis=1)
        staged[n, :, PAIR : 3 * PAIR] = mm(kv_src_t[...], dkv).astype(BF)
        part = nt(dkv, wbuf[b, :, PAIR : 3 * PAIR])
        d_kv_src[...] = part if n == 0 else d_kv_src[...] + part
    dq = jnp.concatenate(dqs, axis=1)
    for n, part in enumerate(lane_pairs(mm(q_src_t[...], dq).astype(BF), count)):
        staged[n, :, :PAIR] = part
    copies = []
    for n in range(count):
        copies += start(store(n))
    d_q_src[...] = nt(dq, columns(wbuf, pairs, 0))
    return copies


def self_fwd_kernel(pieces, n_weights, ints, x_own, x_other, code_in, *refs):
    weights, refs = refs[:n_weights], refs[n_weights:]
    q_ref, k_ref, v_ref, att_ref, logs_ref, mid_ref, normed_t_ref, norms = refs[:8]
    wbuf, own, other, code, normed, mid, q_buf, k_buf, v_buf, att_buf, logs, logs_t, turned, lines, wsems, sems, osems, lsems = refs[8:]
    me = ints[0]
    half = own.shape[0]
    loads = start(moves([(x_own, own), (x_other, other), (code_in, code)], sems))
    blk = wbuf.shape[1] // n_weights
    line_copies = start(
        moves([(w.at[:, pl.ds(blk, PAD), :], lines.at[n]) for n, w in enumerate(weights)], lsems)
    )
    weight_copies = load_weights(me, weights, pieces, wbuf, wsems)
    wait(line_copies)
    parts = jnp.sum(lines[...].astype(F32), axis=(0, 1))
    norms[...] = parts[:8] + parts[8:]
    wait(loads)
    states = own[...].astype(F32)
    mid[...] = states
    normed[:half] = norm_fwd(states, norms[0:1], norms[3:4])
    normed[half:] = norm_fwd(other[...].astype(F32), norms[0:1], norms[3:4])
    wait(weight_copies)
    outs = []

    def emit(n):
        sources = [(q_buf, q_ref), (k_buf, k_ref), (v_buf, v_ref), (att_buf, att_ref)]
        outs.extend(start(moves([(a.at[n], b.at[n]) for a, b in sources], osems.at[n])))

    pairs = list(range(wbuf.shape[0]))
    attention_fwd(
        pairs, normed.at[:half], normed, code.at[:half], code, wbuf, q_buf, k_buf, v_buf, att_buf, logs, mid, emit
    )
    outs.extend(start(moves([(mid, mid_ref)], osems.at[len(pairs)])))
    logs_t[...] = logs[...].T[: logs_t.shape[0]]
    turned[...] = normed[...].T
    outs.extend(start(moves([(logs_t, logs_ref), (turned, normed_t_ref)], osems.at[len(pairs) + 1])))
    wait(outs)


def self_bwd_kernel(pieces, n_weights, pairs, ints, d_mid_in, code_in, q_in, k_in, v_in, att_in, logs_in, normed_t_in, *refs):
    weights, refs = refs[:n_weights], refs[n_weights:]
    d_own_ref, d_other_ref, keep, send = refs[:4]
    wbuf, d_mid, code, q_buf, k_buf, v_buf, att_buf, logs, normed_t, low, low_t, do_buf, d_q, d_kv, d_other, staged, wsems, sems, gsems = refs[4:]
    me = ints[0]
    half = d_mid.shape[0]
    loads = start(
        moves(
            [(d_mid_in, d_mid), (code_in, code), (q_in, q_buf), (k_in, k_buf), (v_in, v_buf), (att_in, att_buf), (logs_in, logs), (normed_t_in, normed_t)],
            sems,
        )
    )
    weight_copies = load_weights(me, weights, pieces, wbuf, wsems)
    wait(loads[:1])
    low[...] = d_mid[...].astype(BF)
    low_t[...] = low[...].T
    wait(loads[1:])
    wait(weight_copies)

    def store(n):
        return store_grad(me, staged, n, keep, send, gsems)

    copies = attention_bwd(
        me, pairs, low, low_t, normed_t.at[:, :half], normed_t, code.at[:half], code, wbuf, q_buf, k_buf, v_buf, att_buf, logs, do_buf, d_q, d_kv, staged, store
    )
    d_other[...] = d_kv[half:].astype(BF)
    outs = start(moves([(d_other, d_other_ref)], sems.at[pl.ds(0, 1)]))
    d_q[...] += d_kv[:half]
    outs += start(moves([(d_q, d_own_ref)], sems.at[pl.ds(1, 1)]))
    wait(outs + copies)


def feed_fwd_kernel(pieces, n_weights, ints, mid_in, norms, *refs):
    weights, refs = refs[:n_weights], refs[n_weights:]
    out_ref, memory_ref, hidden_ref, slope_ref = refs[:4]
    both, mid, out, memory, hidden_buf, slope_buf, normed, wsems, sems, osems = refs[4:]
    me = ints[0]

    @pl.when(ints[1] == 1)
    def _():
        loads = start(moves([(mid_in, mid)], sems))
        weight_copies = load_weights(me, weights, pieces, both, wsems)
        wait(loads)
        normed[...] = norm_fwd(mid[...], norms[1:2], norms[4:5])
        wait(weight_copies)
        outs = []
        ways, _, unit = both.shape
        unit = unit // 2
        for b in range(ways):
            pre = mm(normed[...], both[b, :, :unit])
            cdf, density = gelu_parts(pre)
            hidden_buf[b] = (pre * cdf).astype(BF)
            slope_buf[b] = (cdf + pre * density).astype(BF)
            base = mid[...] if b == 0 else out[...]
            out[...] = base + nt(hidden_buf[b], both[b, :, unit:])
            outs += start(
                moves([(hidden_buf.at[b], hidden_ref.at[b]), (slope_buf.at[b], slope_ref.at[b])], osems.at[b])
            )
        outs += start(moves([(out, out_ref)], osems.at[ways]))
        memory[...] = norm_fwd(out[...], norms[2:3], norms[5:6])
        outs += start(moves([(memory, memory_ref)], sems))
        wait(outs)


def decoder_kernel(pieces, n_weights, ints, mid_in, mem_own, mem_other, code_q_in, code_k_in, cots_in, norms, *refs):
    weights, refs = refs[:n_weights], refs[n_weights:]
    decoded_ref, d_mid_ref, mem_keep, mem_send, small, keep_u, send_u, keep_d, send_d, keep3, send3 = refs[:11]
    (
        wbuf, both, mid, mem, code_q, code_k, cots, cross_in, q_buf, k_buf, v_buf, att_buf, logs, logs_t,
        joined, out, decoded, normed, normed_t, low, low_t, mem_t, do_buf, d_norm, d_q, d_kv, d_mem,
        staged_u, staged_d, staged3, wsems, sems, osems, gsems_u, gsems_d, gsems3,
    ) = refs[11:]
    me = ints[0]
    half = mid.shape[0]

    @pl.when(ints[1] == 0)
    def _():
        loads = start(
            moves(
                [(mid_in, mid), (mem_own, mem.at[:half]), (mem_other, mem.at[half:]), (code_q_in, code_q), (code_k_in, code_k), (cots_in, cots)],
                sems,
            )
        )
        crosses = load_weights(me, weights, pieces[0], wbuf, wsems.at[0])
        feeds = load_weights(me, weights, pieces[1], both, wsems.at[1])
        pairs = list(range(wbuf.shape[0]))
        wait(loads[:1])
        joined[...] = mid[...]
        cross_in[...] = norm_fwd(mid[...], norms[2:3], norms[5:6])
        wait(loads[1:])
        wait(crosses)
        attention_fwd(
            pairs, cross_in, mem, code_q, code_k, wbuf, q_buf, k_buf, v_buf, att_buf, logs, joined, lambda n: None
        )
        logs_t[...] = logs[...].T[: logs_t.shape[0]]
        wait(feeds)
        normed[...] = norm_fwd(joined[...], norms[1:2], norms[4:5])
        normed_t[...] = normed[...].T
        low_t[...] = cots[...].T
        unit = both.shape[2] // 2
        copies = []
        for b in pairs:
            pre = mm(normed[...], both[b, :, :unit])
            cdf, density = gelu_parts(pre)
            hidden = (pre * cdf).astype(BF)
            base = joined[...] if b == 0 else out[...]
            out[...] = base + nt(hidden, both[b, :, unit:])
            d_pre = (mm(cots[...], both[b, :, unit:]) * (cdf + pre * density)).astype(BF)
            staged_u[b] = mm(normed_t[...], d_pre).astype(BF)
            copies += start(store_grad(me, staged_u, b, keep_u, send_u, gsems_u))
            staged_d[b] = mm(low_t[...], hidden).astype(BF)
            copies += start(store_grad(me, staged_d, b, keep_d, send_d, gsems_d))
            part = nt(d_pre, both[b, :, :unit])
            d_norm[...] = part if b == 0 else d_norm[...] + part
        decoded[...] = out[...].astype(BF)
        outs = start(moves([(decoded, decoded_ref)], osems))
        dx, d_gain1, d_bias1 = norm_bwd(joined[...], norms[1:2], d_norm[...])
        joined[...] = cots[...].astype(F32) + dx
        def store3(n):
            return store_grad(me, staged3, n, keep3, send3, gsems3)

        low[...] = joined[...].astype(BF)
        low_t[...] = low[...].T
        mem_t[...] = mem[...].T
        normed_t[...] = cross_in[...].T
        copies += attention_bwd(
            me, pairs, low, low_t, normed_t, mem_t, code_q, code_k, wbuf, q_buf, k_buf, v_buf, att_buf, logs_t, do_buf, d_q, d_kv, staged3, store3
        )
        d_mem[...] = d_kv[...].astype(BF)
        outs += start(
            moves([(d_mem.at[half:], mem_send), (d_mem.at[:half], mem_keep)], osems.at[pl.ds(1, 2)])
        )
        dx, d_gain2, d_bias2 = norm_bwd(mid[...], norms[2:3], d_q[...])
        out[...] = joined[...] + dx
        outs += start(moves([(out, d_mid_ref)], osems.at[pl.ds(3, 1)]))
        small[0:1] = d_gain1
        small[1:2] = d_gain2
        small[2:3] = d_bias1
        small[3:4] = d_bias2
        wait(outs + copies)


def feed_bwd_kernel(pieces, n_weights, ints, encoded_in, mid_in, d_mem_in, cots_in, norms, hidden_in, slope_in, small_in, d_mid_in, keep_u_in, send_u_in, keep_d_in, send_d_in, *refs):
    weights, refs = refs[:n_weights], refs[n_weights:]
    small, d_mid_ref, keep_u, send_u, keep_d, send_d = refs[:6]
    (
        both, encoded, mid, d_mem, cots, hidden, slope, normed_t, low, low_t, d_out, d_norm, staged_u, staged_d, wsems, sems, gsems_u, gsems_d,
    ) = refs[6:]
    me = ints[0]

    @pl.when(ints[1] == 0)
    def _():
        small[...] = small_in[...]

    @pl.when(ints[1] == 1)
    def _():
        loads = start(
            moves(
                [(encoded_in, encoded), (d_mem_in, d_mem), (cots_in, cots), (mid_in, mid), (hidden_in, hidden), (slope_in, slope)],
                sems,
            )
        )
        weight_copies = load_weights(me, weights, pieces, both, wsems)
        wait(loads[:3])
        grad = d_mem[...].astype(F32) + cots[...].astype(F32)
        dx, d_gain, d_bias = norm_bwd(encoded[...], norms[2:3], grad)
        small[1:2] = d_gain
        small[3:4] = d_bias
        d_out[...] = dx
        low[...] = dx.astype(BF)
        low_t[...] = low[...].T
        wait(loads[3:])
        normed_t[...] = norm_fwd(mid[...], norms[1:2], norms[4:5]).T
        wait(weight_copies)
        ways, _, unit = both.shape
        unit = unit // 2
        copies = []
        for b in range(ways):
            d_pre = (mm(low[...], both[b, :, unit:]) * slope[b].astype(F32)).astype(BF)
            staged_u[b] = mm(normed_t[...], d_pre).astype(BF)
            copies += start(store_grad(me, staged_u, b, keep_u, send_u, gsems_u))
            staged_d[b] = mm(low_t[...], hidden[b]).astype(BF)
            copies += start(store_grad(me, staged_d, b, keep_d, send_d, gsems_d))
            part = nt(d_pre, both[b, :, :unit])
            d_norm[...] = part if b == 0 else d_norm[...] + part
        dx, d_gain1, d_bias1 = norm_bwd(mid[...], norms[1:2], d_norm[...])
        d_out[...] += dx
        outs = start(moves([(d_out, d_mid_ref)], sems))
        small[0:1] = d_gain1
        small[2:3] = d_bias1
        wait(outs + copies)


def last_kernel(d_own, d_got, x_own, d_mid, norms, dx_ref, small):
    grad = d_own[...] + d_got[...].astype(F32)
    dx, d_gain, d_bias = norm_bwd(x_own[...].astype(F32), norms[0:1], grad)
    dx_ref[...] = (d_mid[...] + dx).astype(BF)
    small[0:1] = d_gain
    small[1:2] = d_bias


VM = pl.BlockSpec(memory_space=pltpu.VMEM)
SM = pl.BlockSpec(memory_space=pltpu.SMEM)
AN = pl.BlockSpec(memory_space=pl.ANY)


def call(kernel, name, ins, outs, scratch, flops, **more):
    return pl.pallas_call(
        kernel,
        name=name,
        in_specs=[spec for _, spec in ins],
        out_shape=[jax.ShapeDtypeStruct(shape, dtype) for shape, dtype, _ in outs],
        out_specs=[spec for _, _, spec in outs],
        scratch_shapes=scratch,
        compiler_params=pltpu.CompilerParams(vmem_limit_bytes=VMEM_MIB[name] << 20),
        cost_estimate=pl.CostEstimate(flops=flops, bytes_accessed=8 << 20, transcendentals=0),
        **more,
    )(*[array for array, _ in ins])


def on_device(layer_in, segment_ids, out_grads, w_qkv, w_out, w_up, w_down, norm_gain, norm_bias, w_qc, w_kvc, w_oc):
    encoder = lax.axis_index("section") == 0
    me = lax.axis_index("dp")
    core = me & 1
    place = lax.axis_index("mp")
    ways = lax.axis_size("mp")
    count = lax.axis_size("dp")
    rows = layer_in.shape[1]
    width = layer_in.shape[3]
    blk = w_qkv.shape[1]
    half = 2 * layer_in.shape[2]
    length = 2 * half
    assert rows == 2 and ways == 4 and length == segment_ids.shape[2]
    ints = jnp.stack([me, encoder.astype(jnp.int32), place])

    each = norm_gain.shape[2]
    spread = jnp.tile(jnp.concatenate([norm_gain[0], norm_bias[0]]), (1, width // each))
    spread = jnp.where(jnp.arange(width) // each == me * ways + place, spread, 0.0)
    high = spread.astype(BF)
    low = (spread - high.astype(F32)).astype(BF)
    gap = jnp.zeros((2, width), BF)
    shard1 = jnp.concatenate([w_qkv[0].reshape(blk, -1), w_out[0].T], axis=1)
    shard1 = jnp.concatenate([shard1, high, gap, low, gap])
    bits, core_bit = dp_bits(), [1]
    unit = w_up.shape[2]
    shard2 = jnp.concatenate([w_up[0], w_down[0].T], axis=1)
    mine3 = jnp.stack([w_qc, w_kvc[:, 0], w_kvc[:, 1], w_oc.T], axis=1)
    theirs3 = oneway(mine3, "section", 0, 1)
    pair1 = jnp.stack([shard1, swap(shard1, "mp", 2)])
    own2, held2 = shard2[None], [0]
    for bit in bits:
        own2 = jnp.concatenate([own2, swap(own2, "dp", bit)])
        held2 = held2 + [a ^ bit for a in held2]
    up_pair = jnp.stack([w_up[0], swap(w_up[0], "mp", 2)])
    x_own = lax.all_to_all(rows_in(layer_in[0]), "mp", 0, 0, tiled=True).reshape(-1, width)
    cots = lax.all_to_all(after(rows_in(out_grads[0]), x_own), "mp", 0, 0, tiled=True).reshape(-1, width)
    pair1 = after(pair1, x_own)
    all1 = jnp.concatenate([pair1, swap(pair1, "mp", 1)])
    own3 = after(jnp.concatenate([theirs3, mine3], axis=2).reshape(1, blk, -1), pair1)
    for bit in bits:
        own3 = jnp.concatenate([own3, decoder_swap(own3, "dp", bit)])
    w1 = doubled([(all1, 0)], bits)
    up_pair, own2 = after((up_pair, own2), all1)
    up_rest = jnp.concatenate([up_pair[1:], swap(up_pair, "mp", 1)])
    down_own = own2[:, :, unit:]
    down_pair = jnp.stack([down_own, swap(down_own, "mp", 2)])
    up_rest, down_pair = after((up_rest, down_pair), *[w for w, _ in w1])
    w1 = doubled(w1, core_bit)
    x_other = swap(x_own, "dp", 1)

    other_segs = swap(segment_ids, "dp", 1)
    segs = jnp.where(core == (place >> 1), segment_ids, other_segs)
    segs = jnp.where((place & 1) == 0, segs[:, 0], segs[:, 1])
    segs = segs.reshape(2, ways, 2, -1).transpose(0, 2, 1, 3)
    segs = jnp.where(core == 0, segs, segs[:, ::-1]).reshape(2, length)
    lane = jnp.arange(PAIR) & (HD - 1)
    codes = (segs[:, :, None] == lane[None, None, :]).astype(BF)
    code_own = jnp.where(encoder, codes[0], codes[1])

    middle = ways // 2
    dma = pltpu.SemaphoreType.DMA

    def buf(*shape):
        return pltpu.VMEM(shape, BF)

    def fbuf(*shape):
        return pltpu.VMEM(shape, F32)

    def hbm(*arrays):
        return [(a, AN) for a in arrays]

    wbuf = buf(ways, width, 4 * PAIR)
    rows1, every = (pl.ds(0, ways), pl.ds(0, blk)), pl.ds(0, 4 * PAIR)
    pieces1 = [(n, rows1, 0, ways, a, every) for n, (_, a) in enumerate(w1)]

    weights1 = [w for w, _ in w1]

    def kept_shapes(count):
        return [
            ((count, half, PAIR), BF, AN),
            ((count, length, PAIR), BF, AN),
            ((count, length, PAIR), BF, AN),
            ((count, half, PAIR), F32, AN),
            ((8, half), F32, AN),
        ]

    def kept_bufs(count):
        return [buf(count, half, PAIR), buf(count, length, PAIR), buf(count, length, PAIR), fbuf(count, half, PAIR)]

    def grads(pairs, columns):
        return [((count // 2, pairs, blk, columns), BF, AN)] * 2

    state, state_low = ((half, width), F32, AN), ((half, width), BF, AN)

    x_other, cots = together(x_other, cots)
    up_rests = doubled([(up_rest, 0)], bits)
    down_rest = jnp.concatenate([down_pair[1:], swap(down_pair, "mp", 1)])
    pair3 = jnp.stack([own3, decoder_swap(own3, "mp", 2)])
    *kept, mid, normed_t, norms = call(
        functools.partial(self_fwd_kernel, pieces1, len(weights1)),
        "self_fwd",
        [(ints, SM)] + hbm(x_own, x_other, code_own, *weights1),
        kept_shapes(ways) + [state, ((width, length), BF, AN), ((8, width), F32, VM)],
        [wbuf, buf(half, width), buf(half, width), buf(length, PAIR), buf(length, width), fbuf(half, width)]
        + kept_bufs(ways)
        + [fbuf(half, PAIR), fbuf(8, half), buf(width, length), buf(count, ways, PAD, width)]
        + [dma((count,)), dma((3,)), dma((ways + 2, 4)), dma((count,))],
        5 << 30,
    )
    mid, pair3, own2, down_rest, *arrays = together(mid, pair3, own2, down_rest, *[w for w, _ in up_rests])
    up_rests = [(w, a) for w, (_, a) in zip(arrays, up_rests)]
    weights2 = [w for w, _ in doubled([(own2, 0), (down_rest, 0)] + up_rests, core_bit)]
    pieces2 = []
    others, low, high = pl.ds(0, ways - 1), pl.ds(0, unit), pl.ds(unit, unit)
    for n in range(2):
        base = n * (2 + len(up_rests))
        for at, a in enumerate(held2):
            pieces2.append((base, (pl.ds(at, 1),), 0, 1, a ^ n, pl.ds(0, 2 * unit)))
            pieces2.append((base + 1, (others, at), 1, ways - 1, a ^ n, high))
        for at, (_, a) in enumerate(up_rests):
            pieces2.append((base + 2 + at, (others,), 1, ways - 1, a ^ n, low))
    all3 = jnp.concatenate([pair3, decoder_swap(pair3, "mp", 1)])
    wbuf2 = buf(ways, width, 2 * unit)
    encoded, memory, hidden, slope = call(
        functools.partial(feed_fwd_kernel, pieces2, len(weights2)),
        "feed_fwd",
        [(ints, SM)] + hbm(mid) + [(norms, VM)] + hbm(*weights2),
        [state, state_low] + [((ways, half, unit), BF, AN)] * 2,
        [wbuf2, fbuf(half, width), fbuf(half, width), buf(half, width), buf(ways, half, unit), buf(ways, half, unit)]
        + [buf(half, width), dma((3 * count,)), dma((1,)), dma((ways + 1, 2))],
        5 << 30,
    )
    mem_own = oneway(memory, "section", 0, 1)
    mem_other = swap(mem_own, "dp", 1)
    w3 = doubled([(after(all3, mem_own), 0)], core_bit, decoder_swap)
    weights3 = [w for w, _ in w3]
    pieces3 = [(n, (pl.ds(0, ways), at), 0, ways, a ^ n, every) for n in range(2) for at, a in enumerate(held2)]
    dec_pieces = (pieces3, [(len(weights3) + piece[0],) + piece[1:] for piece in pieces2])
    decoded, d_mid, mem_keep, mem_send, small, keep_u, send_u, keep_d, send_d, keep3, send3 = call(
        functools.partial(decoder_kernel, dec_pieces, len(weights3) + len(weights2)),
        "decoder",
        [(ints, SM)] + hbm(mid, mem_own, mem_other, codes[1, :half], codes[0], cots) + [(norms, VM)] + hbm(*weights3, *weights2),
        [state_low, state, state_low, state_low, ((4, width), F32, VM)] + grads(ways, unit) * 2
        + grads(ways, 4 * PAIR),
        [wbuf, wbuf2, fbuf(half, width), buf(length, width), buf(half, PAIR), buf(length, PAIR), buf(half, width)]
        + [buf(half, width)]
        + kept_bufs(ways)
        + [fbuf(half, PAIR), fbuf(8, half), fbuf(half, width), fbuf(half, width), buf(half, width), buf(half, width)]
        + [buf(width, half), buf(half, width), buf(width, half), buf(width, length), buf(ways, half, PAIR)]
        + [fbuf(half, width), fbuf(half, width), fbuf(length, width), buf(length, width)]
        + [buf(ways, width, unit), buf(ways, width, unit), buf(ways, width, 4 * PAIR), dma((2, 3 * count)), dma((6,))]
        + [dma((4,)), dma((ways, count)), dma((ways, count)), dma((ways, count))],
        40 << 30,
    )
    mem_sum = add(mem_keep, swap(mem_send, "dp", 1))
    d_mem = oneway(mem_sum, "section", 1, 0)
    bit = bits[-1]
    got3 = decoder_swap(after(send3, d_mem), "dp", 1)
    keep3, send3 = fold(keep3, got3)
    got3 = decoder_swap(send3, "dp", bit)
    small, d_mid, keep_u, send_u, keep_d, send_d = call(
        functools.partial(feed_bwd_kernel, pieces2, len(weights2)),
        "feed_bwd",
        [(ints, SM)] + hbm(encoded, mid, d_mem, cots) + [(norms, VM)] + hbm(hidden, slope) + [(small, VM)]
        + hbm(d_mid, keep_u, send_u, keep_d, send_d, *weights2),
        [((4, width), F32, VM), state] + grads(ways, unit) * 2,
        [wbuf2, fbuf(half, width), fbuf(half, width), buf(half, width), buf(half, width)]
        + [buf(ways, half, unit), buf(ways, half, unit), buf(width, half), buf(half, width), buf(width, half)]
        + [fbuf(half, width), fbuf(half, width), buf(ways, width, unit), buf(ways, width, unit), dma((3 * count,)), dma((6,))]
        + [dma((ways, count)), dma((ways, count))],
        8 << 30,
        input_output_aliases={9: 1, 10: 2, 11: 3, 12: 4, 13: 5},
    )
    got_u, got_d = swap(send_u, "dp", 1), swap(send_d, "dp", 1)
    section_out = rows_out(jnp.where(encoder, memory, after(decoded, small)))

    def self_bwd(pairs, kept, d_mid):
        return call(
            functools.partial(self_bwd_kernel, pieces1, len(weights1), pairs),
            "self_bwd",
            [(ints, SM)] + hbm(d_mid, code_own, *kept, normed_t, *weights1),
            [state, state_low] + grads(len(pairs), 4 * PAIR),
            [wbuf, fbuf(half, width), buf(length, PAIR)]
            + kept_bufs(len(pairs))
            + [fbuf(8, half), buf(width, length), buf(half, width), buf(width, half), buf(len(pairs), half, PAIR)]
            + [fbuf(half, width), fbuf(length, width), buf(half, width), buf(len(pairs), width, 4 * PAIR)]
            + [dma((count,)), dma((8,)), dma((len(pairs), count))],
            10 << 30,
        )

    got_u, got_d, got3 = together(got_u, got_d, got3)
    keep_u, send_u = fold(keep_u, got_u)
    keep_d, send_d = fold(keep_d, got_d, 1)
    got_u, got_d = swap(send_u, "dp", bit), swap(send_d, "mp", 1)
    keep3, got3 = fold_dp_rest(keep3, got3, decoder_swap)
    keep3, send3 = fold(keep3, got3, 1)
    got3 = decoder_swap(send3, "mp", 1)
    d_own, d_other, keep1, send1 = self_bwd(list(range(ways)), kept, after(d_mid, send_u, send_d, send3))
    d_other, send1, got_u, got_d, got3, section_out = together(
        d_other, send1, got_u, got_d, got3, section_out
    )
    got1 = swap(send1, "dp", 1)
    d_got = swap(d_other, "dp", 1)
    keep3, got3 = fold_mp(keep3, got3, 2, decoder_swap)
    keep1, send1 = fold(keep1, got1)
    keep_u, got_u, keep_d, got_d = after((keep_u, got_u, keep_d, got_d), send1)
    keep_d, send_d = fold(keep_d, got_d)
    got = swap(jnp.concatenate([send1, send_d], axis=1), "dp", bit)
    keep_u, got_u = fold_dp_rest(keep_u, got_u)
    keep_u, send_u = fold(keep_u, got_u, 1)
    got_u = swap(send_u, "mp", 1)
    d_own = after(d_own, send1, send_u, send_d)
    d_x, small0 = call(
        last_kernel,
        "last",
        [(a, VM) for a in (d_own, d_got, x_own, d_mid, norms)],
        [((half, width), BF, VM), ((2, width), F32, VM)],
        [],
        1 << 30,
    )
    in_grads = rows_out(d_x)
    d_x, small0, got, got_u, got3 = together(d_x, small0, got, got_u, got3)
    small = jnp.concatenate([small0[0:1], small[:2], small0[1:2], small[2:]])
    order = relative_order()
    small = small.reshape(6, count, ways, -1).transpose(1, 2, 0, 3)
    small = xor_order(small, me)
    small = xor_order(small.swapaxes(0, 1), place)
    small = jnp.stack([small[n] for n in (0, 2, 1, 3)], axis=1)
    small = jnp.stack([small[a] for a in order])
    for turn in [1] + bits[::-1]:
        small, send = halves(small)
        small = small + swap(send, "dp", turn)
    small = small.reshape(1, ways, 1, -1)
    small = jnp.pad(small, ((0, 0), (0, 0), (0, PAD - 1), (0, 4 * PAIR - small.shape[3])))
    keep1, got1 = fold_dp_rest(keep1, got[:, :ways])
    keep_d, got_d = fold_dp_rest(keep_d, got[:, ways:])
    keep1, send1 = fold(keep1, got1, 1)
    small_keep, small_send = halves(small.astype(BF), 1)
    send1 = jnp.concatenate([send1, small_send], axis=2)
    got1 = swap(send1, "mp", 1)
    keep1 = jnp.concatenate([keep1, small_keep], axis=2)
    r3 = total(keep3, got3).reshape(blk, 4, 2, -1)
    back = oneway(after(r3[:, :, 0].astype(BF), send1), "section", 1, 0)
    keep_u, send_u = fold(keep_u, got_u, 1)
    keep_d, send_d = fold(keep_d, got_d, 1)
    got = swap(jnp.concatenate([send_u, send_d], axis=1), "mp", 2)
    keep1, send1 = fold(keep1, got1, 1)
    got1 = swap(send1, "mp", 2)
    got, back, in_grads, section_out = after((got, back, in_grads, section_out), send1)
    got_u, got_d = halves(got, 1)
    r_up, r_down, r1 = total(keep_u, got_u), total(keep_d, got_d), total(keep1, got1)
    small, r1 = r1[blk, : 6 * each].reshape(6, each), r1[:blk]
    section_out, in_grads = rows_placed(section_out), rows_placed(in_grads)
    grad_qkv = r1[:, : 3 * PAIR].reshape(1, blk, 3, -1)
    grad_out = r1[:, 3 * PAIR :].T[None]
    grad_up = r_up[None]
    grad_down = r_down.T[None]
    r3 = jnp.where(encoder, back.astype(F32), r3[:, :, 1])
    grad_qc, grad_kvc, grad_oc = r3[:, 0], r3[:, 1:3], r3[:, 3].T
    grad_gain = small[None, :3]
    grad_bias = jnp.stack([small[3], small[5]])[None]
    grad_ffn = small[4][None]
    return (
        section_out,
        in_grads,
        grad_qkv,
        grad_out,
        grad_up,
        grad_down,
        grad_gain,
        grad_bias,
        grad_ffn,
        grad_qc,
        grad_kvc,
        grad_oc,
    )


def solution(mesh):
    placed = (
        P("section", "dp", "mp", None),
        P(None, "dp", None),
        P("section", "dp", "mp", None),
        P("section", "dp", None, "mp"),
        P("section", "mp", "dp"),
        P("section", "dp", "mp"),
        P("section", "mp", "dp"),
        P("section", None, ("dp", "mp")),
        P("section", None, ("dp", "mp")),
        P("dp", ("section", "mp")),
        P("dp", None, ("section", "mp")),
        P(("section", "mp"), "dp"),
    )
    return jax.shard_map(
        on_device,
        mesh=mesh,
        in_specs=placed,
        out_specs=(
            P("section", "dp", "mp", None),
            P("section", "dp", "mp", None),
            P("section", "dp", None, "mp"),
            P("section", "mp", "dp"),
            P("section", "dp", "mp"),
            P("section", "mp", "dp"),
            P("section", None, ("dp", "mp")),
            P("section", None, ("dp", "mp")),
            P("section", ("dp", "mp")),
            P("dp", ("section", "mp")),
            P("dp", None, ("section", "mp")),
            P(("section", "mp"), "dp"),
        ),
        check_vma=False,
    )
```

```python
import functools

import jax
import jax.numpy as jnp
from jax import lax
from jax.experimental import pallas as pl
from jax.experimental.pallas import tpu as pltpu
from jax.sharding import PartitionSpec as P

HD = 64
PAIR = 2 * HD
EPS = 1e-05
BIG = 1e30
FACTOR = HD**-0.5
LOG2E = 1.4426950408889634
BF = jnp.bfloat16
F32 = jnp.float32
PAD = 16
VMEM_MIB = {"self_fwd": 56, "feed_fwd": 22, "decoder": 46, "feed_bwd": 56, "self_bwd": 56, "last": 56}


def swap(block, axis, bit):
    count = lax.axis_size(axis)
    return lax.ppermute(block, axis, [(i, i ^ bit) for i in range(count)])


def together(*values):
    return lax.optimization_barrier(values)


def oneway(block, axis, source, target):
    return lax.ppermute(block, axis, [(source, target)])


def dp_bits():
    count = lax.axis_size("dp")
    return [1 << b for b in range(1, count.bit_length() - 1)]


def relative_order():
    order = [0]
    for bit in dp_bits():
        order = order + [a ^ bit for a in order]
    return order + [a ^ 1 for a in order]


def after(x, *others):
    return lax.optimization_barrier((x, others))[0]


def decoder_swap(block, axis, bit):
    count = lax.axis_size(axis)
    pairs = [(count + i, count + (i ^ bit)) for i in range(count)]
    return lax.ppermute(block, ("section", axis), pairs)


def doubled(arrays, bits, move=swap):
    for bit in bits:
        arrays = arrays + [(move(x, "dp", bit), a ^ bit) for x, a in arrays]
    return arrays


def add(a, b):
    return (a.astype(F32) + b.astype(F32)).astype(BF)


def halves(x, axis=0):
    middle = x.shape[axis] // 2
    return lax.slice_in_dim(x, 0, middle, axis=axis), lax.slice_in_dim(x, middle, None, axis=axis)


def fold(keep, got, axis=0):
    (k1, k2), (g1, g2) = halves(keep, axis), halves(got, axis)
    return add(k1, g1), add(k2, g2)


def fold_dp(keep, got, move=swap):
    for bit in dp_bits()[::-1]:
        keep, send = fold(keep, got)
        got = move(send, "dp", bit)
    return keep, got


def fold_dp_rest(keep, got, move=swap):
    for bit in dp_bits()[-2::-1]:
        keep, send = fold(keep, got)
        got = move(send, "dp", bit)
    return keep, got


def fold_mp(keep, got, bit, move=swap):
    keep, send = fold(keep, got, 1)
    return keep, move(send, "mp", bit)


def total(keep, got):
    return keep[0, 0].astype(F32) + got[0, 0].astype(F32)


def rows_in(local):
    rows, span, width = local.shape
    parts = local.reshape(rows, 2, span // 2, width)
    first = (lax.axis_index("dp") & 1) == 0
    keep = jnp.where(first, parts[:, 0], parts[:, 1])
    got = swap(jnp.where(first, parts[:, 1], parts[:, 0]), "dp", 1)
    chip = jnp.where(first, jnp.concatenate([keep, got]), jnp.concatenate([got, keep]))
    return chip


def rows_out(own):
    ways = lax.axis_size("mp")
    return lax.all_to_all(own.reshape(ways, -1, own.shape[1]), "mp", 0, 0, tiled=True)


def rows_placed(chip):
    rows = chip.shape[0] // 2
    first = (lax.axis_index("dp") & 1) == 0
    keep = jnp.where(first, chip[:rows], chip[rows:])
    got = swap(jnp.where(first, chip[rows:], chip[:rows]), "dp", 1)
    return jnp.where(first, jnp.concatenate([keep, got], axis=1), jnp.concatenate([got, keep], axis=1))[None]


def xor_order(x, me):
    count = x.shape[0]
    bit = 1
    while bit < count:
        flipped = x.reshape((count // (2 * bit), 2, bit) + x.shape[1:])[:, ::-1].reshape(x.shape)
        x = jnp.where((me & bit) > 0, flipped, x)
        bit *= 2
    return x


def mm(a, b):
    return jnp.dot(a, b, preferred_element_type=F32)


def nt(a, b):
    return lax.dot_general(a, b, (((1,), (1,)), ((), ())), preferred_element_type=F32)


def stats(states):
    average = jnp.mean(states, axis=-1, keepdims=True)
    centred = states - average
    inv = lax.rsqrt(jnp.mean(centred * centred, axis=-1, keepdims=True) + EPS)
    return centred * inv, inv


def norm_fwd(states, gain, bias):
    hat, _ = stats(states)
    return (hat * gain + bias).astype(BF)


def norm_bwd(states, gain, grad):
    hat, inv = stats(states)
    e = grad * gain
    dx = inv * (
        e - jnp.mean(e, axis=-1, keepdims=True) - hat * jnp.mean(e * hat, axis=-1, keepdims=True)
    )
    return dx, jnp.sum(grad * hat, axis=0, keepdims=True), jnp.sum(grad, axis=0, keepdims=True)


def gelu_parts(pre):
    size = jnp.abs(pre)
    bell = jnp.exp2(pre * pre * (-0.5 * LOG2E))
    t = 1.0 / (1.0 + (0.3275911 * 0.5**0.5) * size)
    poly = 1.061405429 * t - 1.453152027
    poly = poly * t + 1.421413741
    poly = poly * t - 0.284496736
    poly = poly * t + 0.254829592
    tail = 0.5 * poly * t * bell
    return jnp.where(pre >= 0, 1.0 - tail, tail), 0.3989422804014327 * bell


def lanes(rows):
    return lax.broadcasted_iota(jnp.int32, (rows, PAIR), 1)


def head_part(h, real, other):
    lane = lanes(real.shape[0])
    mine = (lane >= HD) if h else (lane < HD)
    return jnp.where(mine, real.astype(F32), other).astype(BF)


def query_code(code):
    return code.astype(F32)


def key_code(code):
    lane = lanes(code.shape[0])
    return jnp.where((lane & (HD - 1)) < 4, (code.astype(F32) - 1.0) * BIG, 0.0)


def start(copies):
    for copy in copies:
        copy.start()
    return copies


def wait(copies):
    for copy in copies:
        copy.wait()


def moves(pairs, sems):
    return [pltpu.make_async_copy(a, b, sems.at[n]) for n, (a, b) in enumerate(pairs)]


def load_weights(me, refs, pieces, target, sems):
    blk = target.shape[1] // len({piece[4] for piece in pieces})
    copies = []
    for n, (ref, index, first, pairs, a, columns) in enumerate(pieces):
        rows = pl.ds(pl.multiple_of((me ^ a) * blk, blk), blk)
        place = target.at[pl.ds(first, pairs), rows, columns]
        copies.append(pltpu.make_async_copy(refs[ref].at[index], place, sems.at[n]))
    return start(copies)


def kernel_order(count):
    order = [0]
    bit = 2
    while bit < count:
        order = order + [a ^ bit for a in order]
        bit *= 2
    return order + [a ^ 1 for a in order]


def store_grad(me, staged, b, keep, send, sems):
    count = 2 * keep.shape[0]
    blk = staged.shape[1] // count
    copies = []
    for n, a in enumerate(kernel_order(count)):
        target = keep.at[n] if n < count // 2 else send.at[n - count // 2]
        rows = pl.ds(pl.multiple_of((me ^ a) * blk, blk), blk)
        copies.append(
            pltpu.make_async_copy(staged.at[b, rows, :], target.at[b], sems.at[b, n])
        )
    return copies


def attend_pair(q, k, v, code_q, code_k, b, logs):
    rows = q.shape[0]
    wide_v = jnp.concatenate([v, jnp.ones_like(v)], axis=1)
    scale = FACTOR * LOG2E
    outs = []
    for h in range(2):
        qa = head_part(h, q, query_code(code_q))
        ka = head_part(h, k, key_code(code_k))
        s = nt(qa, ka)
        top = jnp.max(s, axis=1, keepdims=True)
        p = jnp.exp2((s - top) * scale).astype(BF)
        o = mm(p, wide_v)
        total = o[:, PAIR:]
        outs.append(o[:, :PAIR] / total)
        logs[...] = jnp.where(lanes(rows) == 2 * b + h, top * scale + jnp.log2(total), logs[...])
    return jnp.where(lanes(rows) < HD, outs[0], outs[1])


def attend_pair_back(q, k, v, att, do, code_q, code_k, logs_ref, b):
    rows = q.shape[0]
    scale = FACTOR * LOG2E
    k_t = k.T
    prod = do.astype(F32) * att
    high = prod.astype(BF)
    low = (prod - high.astype(F32)).astype(BF)
    row = lax.broadcasted_iota(jnp.int32, (8, PAIR), 0)
    lane = lax.broadcasted_iota(jnp.int32, (8, PAIR), 1)
    pick = jnp.where((lane // HD) == row, 1.0, 0.0).astype(BF)
    delta = nt(pick, high) + nt(pick, low)
    dk = dv = 0.0
    dq_t = []
    for h in range(2):
        qa = head_part(h, q, query_code(code_q))
        ka = head_part(h, k, key_code(code_k))
        qm = head_part(h, q, 0.0)
        dm = head_part(h, do, 0.0)
        log = logs_ref[pl.ds(2 * b + h, 1), :]
        p_t = jnp.exp2(nt(ka, qa) * scale - log)
        ds_t = (p_t * (nt(v, dm) - delta[h : h + 1])).astype(BF)
        dv = dv + mm(p_t.astype(BF), dm)
        dk = dk + mm(ds_t, qm)
        dq_t.append(mm(k_t, ds_t))
    sub = lax.broadcasted_iota(jnp.int32, (PAIR, rows), 0)
    dq = jnp.where(sub < HD, dq_t[0], dq_t[1]).T
    return (dq * FACTOR).astype(BF), (dk * FACTOR).astype(BF), dv.astype(BF)


def columns(wbuf, pairs, at):
    return jnp.concatenate([wbuf[b, :, at * PAIR : (at + 1) * PAIR] for b in pairs], axis=1)


def lane_pairs(x, count):
    return [x[:, n * PAIR : (n + 1) * PAIR] for n in range(count)]


def attention_fwd(pairs, q_src, kv_src, code_q, code_k, wbuf, q_buf, k_buf, v_buf, att_buf, logs, total, emit):
    count = len(pairs)
    logs[...] = jnp.zeros_like(logs)
    queries = mm(q_src[...], columns(wbuf, pairs, 0)).astype(BF)
    for n, q in enumerate(lane_pairs(queries, count)):
        q_buf[n] = q
    for n, b in enumerate(pairs):
        kv = mm(kv_src[...], wbuf[b, :, PAIR : 3 * PAIR]).astype(BF)
        k_buf[n] = kv[:, :PAIR]
        v_buf[n] = kv[:, PAIR:]
        att_buf[n] = attend_pair(
            q_buf[n], k_buf[n], v_buf[n], code_q[...], code_k[...], n, logs
        )
        emit(n)
    attended = jnp.concatenate([att_buf[n].astype(BF) for n in range(count)], axis=1)
    total[...] += nt(attended, columns(wbuf, pairs, 3))


def attention_bwd(me, pairs, low, low_t, q_src_t, kv_src_t, code_q, code_k, wbuf, q_buf, k_buf, v_buf, att_buf, logs, do_buf, d_q_src, d_kv_src, staged, store):
    count = len(pairs)
    for n, do in enumerate(lane_pairs(mm(low[...], columns(wbuf, pairs, 3)).astype(BF), count)):
        do_buf[n] = do
    attended = jnp.concatenate([att_buf[n].astype(BF) for n in range(count)], axis=1)
    for n, part in enumerate(lane_pairs(mm(low_t[...], attended).astype(BF), count)):
        staged[n, :, 3 * PAIR :] = part
    dqs = []
    for n, b in enumerate(pairs):
        dq, dk, dv = attend_pair_back(
            q_buf[n], k_buf[n], v_buf[n], att_buf[n], do_buf[n], code_q[...], code_k[...], logs, n
        )
        dqs.append(dq)
        dkv = jnp.concatenate([dk, dv], axis=1)
        staged[n, :, PAIR : 3 * PAIR] = mm(kv_src_t[...], dkv).astype(BF)
        part = nt(dkv, wbuf[b, :, PAIR : 3 * PAIR])
        d_kv_src[...] = part if n == 0 else d_kv_src[...] + part
    dq = jnp.concatenate(dqs, axis=1)
    for n, part in enumerate(lane_pairs(mm(q_src_t[...], dq).astype(BF), count)):
        staged[n, :, :PAIR] = part
    copies = []
    for n in range(count):
        copies += start(store(n))
    d_q_src[...] = nt(dq, columns(wbuf, pairs, 0))
    return copies


def self_fwd_kernel(pieces, n_weights, ints, x_own, x_other, code_in, *refs):
    weights, refs = refs[:n_weights], refs[n_weights:]
    q_ref, k_ref, v_ref, att_ref, logs_ref, mid_ref, normed_t_ref, norms = refs[:8]
    wbuf, own, other, code, normed, mid, q_buf, k_buf, v_buf, att_buf, logs, logs_t, turned, lines, wsems, sems, osems, lsems = refs[8:]
    me = ints[0]
    half = own.shape[0]
    loads = start(moves([(x_own, own), (x_other, other), (code_in, code)], sems))
    blk = wbuf.shape[1] // n_weights
    line_copies = start(
        moves([(w.at[:, pl.ds(blk, PAD), :], lines.at[n]) for n, w in enumerate(weights)], lsems)
    )
    weight_copies = load_weights(me, weights, pieces, wbuf, wsems)
    wait(line_copies)
    parts = jnp.sum(lines[...].astype(F32), axis=(0, 1))
    norms[...] = parts[:8] + parts[8:]
    wait(loads)
    states = own[...].astype(F32)
    mid[...] = states
    normed[:half] = norm_fwd(states, norms[0:1], norms[3:4])
    normed[half:] = norm_fwd(other[...].astype(F32), norms[0:1], norms[3:4])
    wait(weight_copies)
    outs = []

    def emit(n):
        sources = [(q_buf, q_ref), (k_buf, k_ref), (v_buf, v_ref), (att_buf, att_ref)]
        outs.extend(start(moves([(a.at[n], b.at[n]) for a, b in sources], osems.at[n])))

    pairs = list(range(wbuf.shape[0]))
    attention_fwd(
        pairs, normed.at[:half], normed, code.at[:half], code, wbuf, q_buf, k_buf, v_buf, att_buf, logs, mid, emit
    )
    outs.extend(start(moves([(mid, mid_ref)], osems.at[len(pairs)])))
    logs_t[...] = logs[...].T[: logs_t.shape[0]]
    turned[...] = normed[...].T
    outs.extend(start(moves([(logs_t, logs_ref), (turned, normed_t_ref)], osems.at[len(pairs) + 1])))
    wait(outs)


def self_bwd_kernel(pieces, n_weights, pairs, ints, d_mid_in, code_in, q_in, k_in, v_in, att_in, logs_in, normed_t_in, *refs):
    weights, refs = refs[:n_weights], refs[n_weights:]
    d_own_ref, d_other_ref, keep, send = refs[:4]
    wbuf, d_mid, code, q_buf, k_buf, v_buf, att_buf, logs, normed_t, low, low_t, do_buf, d_q, d_kv, d_other, staged, wsems, sems, gsems = refs[4:]
    me = ints[0]
    half = d_mid.shape[0]
    loads = start(
        moves(
            [(d_mid_in, d_mid), (code_in, code), (q_in, q_buf), (k_in, k_buf), (v_in, v_buf), (att_in, att_buf), (logs_in, logs), (normed_t_in, normed_t)],
            sems,
        )
    )
    weight_copies = load_weights(me, weights, pieces, wbuf, wsems)
    wait(loads[:1])
    low[...] = d_mid[...].astype(BF)
    low_t[...] = low[...].T
    wait(loads[1:])
    wait(weight_copies)

    def store(n):
        return store_grad(me, staged, n, keep, send, gsems)

    copies = attention_bwd(
        me, pairs, low, low_t, normed_t.at[:, :half], normed_t, code.at[:half], code, wbuf, q_buf, k_buf, v_buf, att_buf, logs, do_buf, d_q, d_kv, staged, store
    )
    d_other[...] = d_kv[half:].astype(BF)
    outs = start(moves([(d_other, d_other_ref)], sems.at[pl.ds(0, 1)]))
    d_q[...] += d_kv[:half]
    outs += start(moves([(d_q, d_own_ref)], sems.at[pl.ds(1, 1)]))
    wait(outs + copies)


def feed_fwd_kernel(pieces, n_weights, ints, mid_in, norms, *refs):
    weights, refs = refs[:n_weights], refs[n_weights:]
    out_ref, memory_ref, hidden_ref, slope_ref = refs[:4]
    both, mid, out, memory, hidden_buf, slope_buf, normed, wsems, sems, osems = refs[4:]
    me = ints[0]

    @pl.when(ints[1] == 1)
    def _():
        loads = start(moves([(mid_in, mid)], sems))
        weight_copies = load_weights(me, weights, pieces, both, wsems)
        wait(loads)
        normed[...] = norm_fwd(mid[...], norms[1:2], norms[4:5])
        wait(weight_copies)
        outs = []
        ways, _, unit = both.shape
        unit = unit // 2
        for b in range(ways):
            pre = mm(normed[...], both[b, :, :unit])
            cdf, density = gelu_parts(pre)
            hidden_buf[b] = (pre * cdf).astype(BF)
            slope_buf[b] = (cdf + pre * density).astype(BF)
            base = mid[...] if b == 0 else out[...]
            out[...] = base + nt(hidden_buf[b], both[b, :, unit:])
            outs += start(
                moves([(hidden_buf.at[b], hidden_ref.at[b]), (slope_buf.at[b], slope_ref.at[b])], osems.at[b])
            )
        outs += start(moves([(out, out_ref)], osems.at[ways]))
        memory[...] = norm_fwd(out[...], norms[2:3], norms[5:6])
        outs += start(moves([(memory, memory_ref)], sems))
        wait(outs)


def decoder_kernel(pieces, n_weights, ints, mid_in, mem_own, mem_other, code_q_in, code_k_in, cots_in, norms, *refs):
    weights, refs = refs[:n_weights], refs[n_weights:]
    decoded_ref, d_mid_ref, mem_keep, mem_send, small, keep_u, send_u, keep_d, send_d, keep3, send3 = refs[:11]
    (
        wbuf, both, mid, mem, code_q, code_k, cots, cross_in, q_buf, k_buf, v_buf, att_buf, logs, logs_t,
        joined, out, decoded, normed, normed_t, low, low_t, mem_t, do_buf, d_norm, d_q, d_kv, d_mem,
        staged_u, staged_d, staged3, wsems, sems, osems, gsems_u, gsems_d, gsems3,
    ) = refs[11:]
    me = ints[0]
    half = mid.shape[0]

    @pl.when(ints[1] == 0)
    def _():
        loads = start(
            moves(
                [(mid_in, mid), (mem_own, mem.at[:half]), (mem_other, mem.at[half:]), (code_q_in, code_q), (code_k_in, code_k), (cots_in, cots)],
                sems,
            )
        )
        crosses = load_weights(me, weights, pieces[0], wbuf, wsems.at[0])
        feeds = load_weights(me, weights, pieces[1], both, wsems.at[1])
        pairs = list(range(wbuf.shape[0]))
        wait(loads[:1])
        joined[...] = mid[...]
        cross_in[...] = norm_fwd(mid[...], norms[2:3], norms[5:6])
        wait(loads[1:])
        wait(crosses)
        attention_fwd(
            pairs, cross_in, mem, code_q, code_k, wbuf, q_buf, k_buf, v_buf, att_buf, logs, joined, lambda n: None
        )
        logs_t[...] = logs[...].T[: logs_t.shape[0]]
        wait(feeds)
        normed[...] = norm_fwd(joined[...], norms[1:2], norms[4:5])
        normed_t[...] = normed[...].T
        low_t[...] = cots[...].T
        unit = both.shape[2] // 2
        copies = []
        for b in pairs:
            pre = mm(normed[...], both[b, :, :unit])
            cdf, density = gelu_parts(pre)
            hidden = (pre * cdf).astype(BF)
            base = joined[...] if b == 0 else out[...]
            out[...] = base + nt(hidden, both[b, :, unit:])
            d_pre = (mm(cots[...], both[b, :, unit:]) * (cdf + pre * density)).astype(BF)
            staged_u[b] = mm(normed_t[...], d_pre).astype(BF)
            copies += start(store_grad(me, staged_u, b, keep_u, send_u, gsems_u))
            staged_d[b] = mm(low_t[...], hidden).astype(BF)
            copies += start(store_grad(me, staged_d, b, keep_d, send_d, gsems_d))
            part = nt(d_pre, both[b, :, :unit])
            d_norm[...] = part if b == 0 else d_norm[...] + part
        decoded[...] = out[...].astype(BF)
        outs = start(moves([(decoded, decoded_ref)], osems))
        dx, d_gain1, d_bias1 = norm_bwd(joined[...], norms[1:2], d_norm[...])
        joined[...] = cots[...].astype(F32) + dx
        def store3(n):
            return store_grad(me, staged3, n, keep3, send3, gsems3)

        low[...] = joined[...].astype(BF)
        low_t[...] = low[...].T
        mem_t[...] = mem[...].T
        normed_t[...] = cross_in[...].T
        copies += attention_bwd(
            me, pairs, low, low_t, normed_t, mem_t, code_q, code_k, wbuf, q_buf, k_buf, v_buf, att_buf, logs_t, do_buf, d_q, d_kv, staged3, store3
        )
        d_mem[...] = d_kv[...].astype(BF)
        outs += start(
            moves([(d_mem.at[half:], mem_send), (d_mem.at[:half], mem_keep)], osems.at[pl.ds(1, 2)])
        )
        dx, d_gain2, d_bias2 = norm_bwd(mid[...], norms[2:3], d_q[...])
        out[...] = joined[...] + dx
        outs += start(moves([(out, d_mid_ref)], osems.at[pl.ds(3, 1)]))
        small[0:1] = d_gain1
        small[1:2] = d_gain2
        small[2:3] = d_bias1
        small[3:4] = d_bias2
        wait(outs + copies)


def feed_bwd_kernel(pieces, n_weights, ints, encoded_in, mid_in, d_mem_in, cots_in, norms, hidden_in, slope_in, small_in, d_mid_in, keep_u_in, send_u_in, keep_d_in, send_d_in, *refs):
    weights, refs = refs[:n_weights], refs[n_weights:]
    small, d_mid_ref, keep_u, send_u, keep_d, send_d = refs[:6]
    (
        both, encoded, mid, d_mem, cots, hidden, slope, normed_t, low, low_t, d_out, d_norm, staged_u, staged_d, wsems, sems, gsems_u, gsems_d,
    ) = refs[6:]
    me = ints[0]

    @pl.when(ints[1] == 0)
    def _():
        small[...] = small_in[...]

    @pl.when(ints[1] == 1)
    def _():
        loads = start(
            moves(
                [(encoded_in, encoded), (d_mem_in, d_mem), (cots_in, cots), (mid_in, mid), (hidden_in, hidden), (slope_in, slope)],
                sems,
            )
        )
        weight_copies = load_weights(me, weights, pieces, both, wsems)
        wait(loads[:3])
        grad = d_mem[...].astype(F32) + cots[...].astype(F32)
        dx, d_gain, d_bias = norm_bwd(encoded[...], norms[2:3], grad)
        small[1:2] = d_gain
        small[3:4] = d_bias
        d_out[...] = dx
        low[...] = dx.astype(BF)
        low_t[...] = low[...].T
        wait(loads[3:])
        normed_t[...] = norm_fwd(mid[...], norms[1:2], norms[4:5]).T
        wait(weight_copies)
        ways, _, unit = both.shape
        unit = unit // 2
        copies = []
        for b in range(ways):
            d_pre = (mm(low[...], both[b, :, unit:]) * slope[b].astype(F32)).astype(BF)
            staged_u[b] = mm(normed_t[...], d_pre).astype(BF)
            copies += start(store_grad(me, staged_u, b, keep_u, send_u, gsems_u))
            staged_d[b] = mm(low_t[...], hidden[b]).astype(BF)
            copies += start(store_grad(me, staged_d, b, keep_d, send_d, gsems_d))
            part = nt(d_pre, both[b, :, :unit])
            d_norm[...] = part if b == 0 else d_norm[...] + part
        dx, d_gain1, d_bias1 = norm_bwd(mid[...], norms[1:2], d_norm[...])
        d_out[...] += dx
        outs = start(moves([(d_out, d_mid_ref)], sems))
        small[0:1] = d_gain1
        small[2:3] = d_bias1
        wait(outs + copies)


def last_kernel(d_own, d_got, x_own, d_mid, norms, dx_ref, small):
    grad = d_own[...] + d_got[...].astype(F32)
    dx, d_gain, d_bias = norm_bwd(x_own[...].astype(F32), norms[0:1], grad)
    dx_ref[...] = (d_mid[...] + dx).astype(BF)
    small[0:1] = d_gain
    small[1:2] = d_bias


VM = pl.BlockSpec(memory_space=pltpu.VMEM)
SM = pl.BlockSpec(memory_space=pltpu.SMEM)
AN = pl.BlockSpec(memory_space=pl.ANY)


def call(kernel, name, ins, outs, scratch, flops, **more):
    return pl.pallas_call(
        kernel,
        name=name,
        in_specs=[spec for _, spec in ins],
        out_shape=[jax.ShapeDtypeStruct(shape, dtype) for shape, dtype, _ in outs],
        out_specs=[spec for _, _, spec in outs],
        scratch_shapes=scratch,
        compiler_params=pltpu.CompilerParams(vmem_limit_bytes=VMEM_MIB[name] << 20),
        cost_estimate=pl.CostEstimate(flops=flops, bytes_accessed=8 << 20, transcendentals=0),
        **more,
    )(*[array for array, _ in ins])


def on_device(layer_in, segment_ids, out_grads, w_qkv, w_out, w_up, w_down, norm_gain, norm_bias, w_qc, w_kvc, w_oc):
    encoder = lax.axis_index("section") == 0
    me = lax.axis_index("dp")
    core = me & 1
    place = lax.axis_index("mp")
    ways = lax.axis_size("mp")
    count = lax.axis_size("dp")
    rows = layer_in.shape[1]
    width = layer_in.shape[3]
    blk = w_qkv.shape[1]
    half = 2 * layer_in.shape[2]
    length = 2 * half
    assert rows == 2 and ways == 4 and length == segment_ids.shape[2]
    ints = jnp.stack([me, encoder.astype(jnp.int32), place])

    each = norm_gain.shape[2]
    spread = jnp.tile(jnp.concatenate([norm_gain[0], norm_bias[0]]), (1, width // each))
    spread = jnp.where(jnp.arange(width) // each == me * ways + place, spread, 0.0)
    high = spread.astype(BF)
    low = (spread - high.astype(F32)).astype(BF)
    gap = jnp.zeros((2, width), BF)
    shard1 = jnp.concatenate([w_qkv[0].reshape(blk, -1), w_out[0].T], axis=1)
    shard1 = jnp.concatenate([shard1, high, gap, low, gap])
    bits, core_bit = dp_bits(), [1]
    unit = w_up.shape[2]
    shard2 = jnp.concatenate([w_up[0], w_down[0].T], axis=1)
    mine3 = jnp.stack([w_qc, w_kvc[:, 0], w_kvc[:, 1], w_oc.T], axis=1)
    theirs3 = oneway(mine3, "section", 0, 1)
    pair1 = jnp.stack([shard1, swap(shard1, "mp", 2)])
    own2, held2 = shard2[None], [0]
    for bit in bits:
        own2 = jnp.concatenate([own2, swap(own2, "dp", bit)])
        held2 = held2 + [a ^ bit for a in held2]
    up_pair = jnp.stack([w_up[0], swap(w_up[0], "mp", 2)])
    x_own = lax.all_to_all(rows_in(layer_in[0]), "mp", 0, 0, tiled=True).reshape(-1, width)
    cots = lax.all_to_all(after(rows_in(out_grads[0]), x_own), "mp", 0, 0, tiled=True).reshape(-1, width)
    pair1 = after(pair1, x_own)
    all1 = jnp.concatenate([pair1, swap(pair1, "mp", 1)])
    own3 = after(jnp.concatenate([theirs3, mine3], axis=2).reshape(1, blk, -1), pair1)
    for bit in bits:
        own3 = jnp.concatenate([own3, decoder_swap(own3, "dp", bit)])
    w1 = doubled([(all1, 0)], bits)
    up_pair, own2 = after(up_pair, all1), after(own2, x_own)
    up_rest = jnp.concatenate([up_pair[1:], swap(up_pair, "mp", 1)])
    down_own = own2[:, :, unit:]
    down_pair = jnp.stack([down_own, swap(down_own, "mp", 2)])
    w1 = [(after(w, up_rest), a) for w, a in w1]
    w1 = doubled(w1, core_bit)
    x_other = swap(x_own, "dp", 1)

    other_segs = swap(segment_ids, "dp", 1)
    segs = jnp.where(core == (place >> 1), segment_ids, other_segs)
    segs = jnp.where((place & 1) == 0, segs[:, 0], segs[:, 1])
    segs = segs.reshape(2, ways, 2, -1).transpose(0, 2, 1, 3)
    segs = jnp.where(core == 0, segs, segs[:, ::-1]).reshape(2, length)
    lane = jnp.arange(PAIR) & (HD - 1)
    codes = (segs[:, :, None] == lane[None, None, :]).astype(BF)
    code_own = jnp.where(encoder, codes[0], codes[1])

    middle = ways // 2
    dma = pltpu.SemaphoreType.DMA

    def buf(*shape):
        return pltpu.VMEM(shape, BF)

    def fbuf(*shape):
        return pltpu.VMEM(shape, F32)

    def hbm(*arrays):
        return [(a, AN) for a in arrays]

    wbuf = buf(ways, width, 4 * PAIR)
    rows1, every = (pl.ds(0, ways), pl.ds(0, blk)), pl.ds(0, 4 * PAIR)
    pieces1 = [(n, rows1, 0, ways, a, every) for n, (_, a) in enumerate(w1)]

    weights1 = [w for w, _ in w1]

    def kept_shapes(count):
        return [
            ((count, half, PAIR), BF, AN),
            ((count, length, PAIR), BF, AN),
            ((count, length, PAIR), BF, AN),
            ((count, half, PAIR), F32, AN),
            ((8, half), F32, AN),
        ]

    def kept_bufs(count):
        return [buf(count, half, PAIR), buf(count, length, PAIR), buf(count, length, PAIR), fbuf(count, half, PAIR)]

    def grads(pairs, columns):
        return [((count // 2, pairs, blk, columns), BF, AN)] * 2

    state, state_low = ((half, width), F32, AN), ((half, width), BF, AN)

    up_rests = doubled([(up_rest, 0)], bits)
    down_rest = jnp.concatenate([down_pair[1:], swap(down_pair, "mp", 1)])
    pair3 = jnp.stack([own3, decoder_swap(own3, "mp", 2)])
    *kept, mid, normed_t, norms = call(
        functools.partial(self_fwd_kernel, pieces1, len(weights1)),
        "self_fwd",
        [(ints, SM)] + hbm(x_own, x_other, code_own, *weights1),
        kept_shapes(ways) + [state, ((width, length), BF, AN), ((8, width), F32, VM)],
        [wbuf, buf(half, width), buf(half, width), buf(length, PAIR), buf(length, width), fbuf(half, width)]
        + kept_bufs(ways)
        + [fbuf(half, PAIR), fbuf(8, half), buf(width, length), buf(count, ways, PAD, width)]
        + [dma((count,)), dma((3,)), dma((ways + 2, 4)), dma((count,))],
        5 << 30,
    )
    mid, cots, pair3, own2, down_rest, *arrays = together(
        mid, cots, pair3, own2, down_rest, *[w for w, _ in up_rests]
    )
    up_rests = [(w, a) for w, (_, a) in zip(arrays, up_rests)]
    weights2 = [w for w, _ in doubled([(own2, 0), (down_rest, 0)] + up_rests, core_bit)]
    pieces2 = []
    others, low, high = pl.ds(0, ways - 1), pl.ds(0, unit), pl.ds(unit, unit)
    for n in range(2):
        base = n * (2 + len(up_rests))
        for at, a in enumerate(held2):
            pieces2.append((base, (pl.ds(at, 1),), 0, 1, a ^ n, pl.ds(0, 2 * unit)))
            pieces2.append((base + 1, (others, at), 1, ways - 1, a ^ n, high))
        for at, (_, a) in enumerate(up_rests):
            pieces2.append((base + 2 + at, (others,), 1, ways - 1, a ^ n, low))
    all3 = jnp.concatenate([pair3, decoder_swap(pair3, "mp", 1)])
    wbuf2 = buf(ways, width, 2 * unit)
    encoded, memory, hidden, slope = call(
        functools.partial(feed_fwd_kernel, pieces2, len(weights2)),
        "feed_fwd",
        [(ints, SM)] + hbm(mid) + [(norms, VM)] + hbm(*weights2),
        [state, state_low] + [((ways, half, unit), BF, AN)] * 2,
        [wbuf2, fbuf(half, width), fbuf(half, width), buf(half, width), buf(ways, half, unit), buf(ways, half, unit)]
        + [buf(half, width), dma((3 * count,)), dma((1,)), dma((ways + 1, 2))],
        5 << 30,
    )
    mem_own = oneway(memory, "section", 0, 1)
    mem_other = swap(mem_own, "dp", 1)
    w3 = doubled([(after(all3, mem_own), 0)], core_bit, decoder_swap)
    weights3 = [w for w, _ in w3]
    pieces3 = [(n, (pl.ds(0, ways), at), 0, ways, a ^ n, every) for n in range(2) for at, a in enumerate(held2)]
    dec_pieces = (pieces3, [(len(weights3) + piece[0],) + piece[1:] for piece in pieces2])
    decoded, d_mid, mem_keep, mem_send, small, keep_u, send_u, keep_d, send_d, keep3, send3 = call(
        functools.partial(decoder_kernel, dec_pieces, len(weights3) + len(weights2)),
        "decoder",
        [(ints, SM)] + hbm(mid, mem_own, mem_other, codes[1, :half], codes[0], cots) + [(norms, VM)] + hbm(*weights3, *weights2),
        [state_low, state, state_low, state_low, ((4, width), F32, VM)] + grads(ways, unit) * 2
        + grads(ways, 4 * PAIR),
        [wbuf, wbuf2, fbuf(half, width), buf(length, width), buf(half, PAIR), buf(length, PAIR), buf(half, width)]
        + [buf(half, width)]
        + kept_bufs(ways)
        + [fbuf(half, PAIR), fbuf(8, half), fbuf(half, width), fbuf(half, width), buf(half, width), buf(half, width)]
        + [buf(width, half), buf(half, width), buf(width, half), buf(width, length), buf(ways, half, PAIR)]
        + [fbuf(half, width), fbuf(half, width), fbuf(length, width), buf(length, width)]
        + [buf(ways, width, unit), buf(ways, width, unit), buf(ways, width, 4 * PAIR), dma((2, 3 * count)), dma((6,))]
        + [dma((4,)), dma((ways, count)), dma((ways, count)), dma((ways, count))],
        40 << 30,
    )
    mem_sum = add(mem_keep, swap(mem_send, "dp", 1))
    d_mem = oneway(mem_sum, "section", 1, 0)
    bit = bits[-1]
    got3 = decoder_swap(after(send3, d_mem), "dp", 1)
    keep3, send3 = fold(keep3, got3)
    got3 = decoder_swap(send3, "dp", bit)
    small, d_mid, keep_u, send_u, keep_d, send_d = call(
        functools.partial(feed_bwd_kernel, pieces2, len(weights2)),
        "feed_bwd",
        [(ints, SM)] + hbm(encoded, mid, d_mem, cots) + [(norms, VM)] + hbm(hidden, slope) + [(small, VM)]
        + hbm(d_mid, keep_u, send_u, keep_d, send_d, *weights2),
        [((4, width), F32, VM), state] + grads(ways, unit) * 2,
        [wbuf2, fbuf(half, width), fbuf(half, width), buf(half, width), buf(half, width)]
        + [buf(ways, half, unit), buf(ways, half, unit), buf(width, half), buf(half, width), buf(width, half)]
        + [fbuf(half, width), fbuf(half, width), buf(ways, width, unit), buf(ways, width, unit), dma((3 * count,)), dma((6,))]
        + [dma((ways, count)), dma((ways, count))],
        8 << 30,
        input_output_aliases={9: 1, 10: 2, 11: 3, 12: 4, 13: 5},
    )
    got_u, got_d = swap(send_u, "dp", 1), swap(send_d, "dp", 1)
    section_out = rows_out(jnp.where(encoder, memory, after(decoded, small)))

    def self_bwd(pairs, kept, d_mid):
        return call(
            functools.partial(self_bwd_kernel, pieces1, len(weights1), pairs),
            "self_bwd",
            [(ints, SM)] + hbm(d_mid, code_own, *kept, normed_t, *weights1),
            [state, state_low] + grads(len(pairs), 4 * PAIR),
            [wbuf, fbuf(half, width), buf(length, PAIR)]
            + kept_bufs(len(pairs))
            + [fbuf(8, half), buf(width, length), buf(half, width), buf(width, half), buf(len(pairs), half, PAIR)]
            + [fbuf(half, width), fbuf(length, width), buf(half, width), buf(len(pairs), width, 4 * PAIR)]
            + [dma((count,)), dma((8,)), dma((len(pairs), count))],
            10 << 30,
        )

    got_u, got_d, got3 = together(got_u, got_d, got3)
    keep_u, send_u = fold(keep_u, got_u)
    keep_d, send_d = fold(keep_d, got_d, 1)
    got_u, got_d = swap(send_u, "dp", bit), swap(send_d, "mp", 1)
    keep3, got3 = fold_dp_rest(keep3, got3, decoder_swap)
    keep3, send3 = fold(keep3, got3, 1)
    got3 = decoder_swap(send3, "mp", 1)
    d_own, d_other, keep1, send1 = self_bwd(list(range(ways)), kept, after(d_mid, send_u, send_d, send3))
    d_other, send1, got_u, got_d, got3, section_out = together(
        d_other, send1, got_u, got_d, got3, section_out
    )
    got1 = swap(send1, "dp", 1)
    d_got = swap(d_other, "dp", 1)
    keep3, got3 = fold_mp(keep3, got3, 2, decoder_swap)
    keep1, send1 = fold(keep1, got1)
    keep_u, got_u, keep_d, got_d = after((keep_u, got_u, keep_d, got_d), send1)
    keep_d, send_d = fold(keep_d, got_d)
    got = swap(jnp.concatenate([send1, send_d], axis=1), "dp", bit)
    keep_u, got_u = fold_dp_rest(keep_u, got_u)
    keep_u, send_u = fold(keep_u, got_u, 1)
    got_u = swap(send_u, "mp", 1)
    d_own = after(d_own, send1, send_u, send_d)
    d_x, small0 = call(
        last_kernel,
        "last",
        [(a, VM) for a in (d_own, d_got, x_own, d_mid, norms)],
        [((half, width), BF, VM), ((2, width), F32, VM)],
        [],
        1 << 30,
    )
    in_grads = rows_out(d_x)
    d_x, small0, got, got_u, got3 = together(d_x, small0, got, got_u, got3)
    small = jnp.concatenate([small0[0:1], small[:2], small0[1:2], small[2:]])
    order = relative_order()
    small = small.reshape(6, count, ways, -1).transpose(1, 2, 0, 3)
    small = xor_order(small, me)
    small = xor_order(small.swapaxes(0, 1), place)
    small = jnp.stack([small[n] for n in (0, 2, 1, 3)], axis=1)
    small = jnp.stack([small[a] for a in order])
    for turn in [1] + bits[::-1]:
        small, send = halves(small)
        small = small + swap(send, "dp", turn)
    small = small.reshape(1, ways, 1, -1)
    small = jnp.pad(small, ((0, 0), (0, 0), (0, PAD - 1), (0, 4 * PAIR - small.shape[3])))
    keep1, got1 = fold_dp_rest(keep1, got[:, :ways])
    keep_d, got_d = fold_dp_rest(keep_d, got[:, ways:])
    keep1, send1 = fold(keep1, got1, 1)
    small_keep, small_send = halves(small.astype(BF), 1)
    send1 = jnp.concatenate([send1, small_send], axis=2)
    got1 = swap(send1, "mp", 1)
    keep1 = jnp.concatenate([keep1, small_keep], axis=2)
    r3 = total(keep3, got3).reshape(blk, 4, 2, -1)
    back = oneway(after(r3[:, :, 0].astype(BF), send1), "section", 1, 0)
    keep_u, send_u = fold(keep_u, got_u, 1)
    keep_d, send_d = fold(keep_d, got_d, 1)
    got = swap(jnp.concatenate([send_u, send_d], axis=1), "mp", 2)
    keep1, send1 = fold(keep1, got1, 1)
    got1 = swap(send1, "mp", 2)
    got, back, in_grads, section_out = after((got, back, in_grads, section_out), send1)
    got_u, got_d = halves(got, 1)
    r_up, r_down, r1 = total(keep_u, got_u), total(keep_d, got_d), total(keep1, got1)
    small, r1 = r1[blk, : 6 * each].reshape(6, each), r1[:blk]
    section_out, in_grads = rows_placed(section_out), rows_placed(in_grads)
    grad_qkv = r1[:, : 3 * PAIR].reshape(1, blk, 3, -1)
    grad_out = r1[:, 3 * PAIR :].T[None]
    grad_up = r_up[None]
    grad_down = r_down.T[None]
    r3 = jnp.where(encoder, back.astype(F32), r3[:, :, 1])
    grad_qc, grad_kvc, grad_oc = r3[:, 0], r3[:, 1:3], r3[:, 3].T
    grad_gain = small[None, :3]
    grad_bias = jnp.stack([small[3], small[5]])[None]
    grad_ffn = small[4][None]
    return (
        section_out,
        in_grads,
        grad_qkv,
        grad_out,
        grad_up,
        grad_down,
        grad_gain,
        grad_bias,
        grad_ffn,
        grad_qc,
        grad_kvc,
        grad_oc,
    )


def solution(mesh):
    placed = (
        P("section", "dp", "mp", None),
        P(None, "dp", None),
        P("section", "dp", "mp", None),
        P("section", "dp", None, "mp"),
        P("section", "mp", "dp"),
        P("section", "dp", "mp"),
        P("section", "mp", "dp"),
        P("section", None, ("dp", "mp")),
        P("section", None, ("dp", "mp")),
        P("dp", ("section", "mp")),
        P("dp", None, ("section", "mp")),
        P(("section", "mp"), "dp"),
    )
    return jax.shard_map(
        on_device,
        mesh=mesh,
        in_specs=placed,
        out_specs=(
            P("section", "dp", "mp", None),
            P("section", "dp", "mp", None),
            P("section", "dp", None, "mp"),
            P("section", "mp", "dp"),
            P("section", "dp", "mp"),
            P("section", "mp", "dp"),
            P("section", None, ("dp", "mp")),
            P("section", None, ("dp", "mp")),
            P("section", ("dp", "mp")),
            P("dp", ("section", "mp")),
            P("dp", None, ("section", "mp")),
            P(("section", "mp"), "dp"),
        ),
        check_vma=False,
    )
```
